256 devices in a mesh: rows: 64 (over y, z, core), cents: 4 (over x).
Axes of the slice: x: 4, y: 4, z: 8, core: 2. Of those that a mesh axis runs over, the one named last changes fastest.
Arguments:
- patients: bfloat16 [131072, 256], P('rows')
- centroids: bfloat16 [8192, 256], P('cents'), as said below
Outputs:
- new_centroids: float32 [8192, 256], P('cents')
- log_scale: float32 [131072], P('rows')
Inputs may be any that keep to these rules, and one draw needn't show every extreme that they name: `centroids`: centroid embeddings.
All inputs are finite; a program needn't handle non-finite values.
Results may differ from the reference program's by a relative error of at most 0.002.
Values sent between devices are 32-bit elements; how exact they have to be, the bound alone decides.
A program may use at most 64 MiB of HBM per device.

```python
import jax
import jax.numpy as jnp
from jax import lax

D = 256
ROW_DEV = 2048
ITERS = 3
ROWS = 131072
K = 8192


def centroid_rows(key):
    base = jax.random.normal(jax.random.fold_in(key, 100), (K, D), jnp.float32) * 0.0625
    return base


def draw_centroids(key, part):
    full = centroid_rows(key)
    return full.astype(jnp.bfloat16)


def draw_patients(key, part):
    key = jax.random.fold_in(key, 2)
    base = jax.random.normal(key, (ROWS, D), jnp.float32) * 0.0625
    result = base
    return result.astype(jnp.bfloat16)


def setup_inputs(seed: int = 0) -> dict:
    key_of = jax.random.split(jax.random.key(seed), 3)
    patients = draw_patients(jax.random.fold_in(key_of[2], 71), 0)
    centroids = draw_centroids(jax.random.fold_in(key_of[2], 71), 0)
    return {"patients": patients, "centroids": centroids}


TAU = 0.05


def block_expo(block, centroids, norms):
    logits = (2.0 * jnp.dot(block, centroids.T, preferred_element_type=jnp.float32) - norms[None, :]) / TAU
    peak = jnp.max(logits, axis=1, keepdims=True)
    return jnp.exp(logits - peak)


def reference(patients, centroids):
    cent_f = centroids.astype(jnp.float32)
    norms = jnp.sum(cent_f * cent_f, axis=1)
    blocks = patients.reshape(ROWS // ROW_DEV, ROW_DEV, D)
    ratio = jnp.float32(ROWS / K)

    def first_pass(carry, block):
        expo = block_expo(block, centroids, norms)
        return carry + jnp.sum(expo, axis=0), None

    column_mass, unused = lax.scan(first_pass, jnp.zeros((K,), jnp.float32), blocks)
    col_scale = ratio / jnp.maximum(column_mass, 1.0)
    for step in range(ITERS):
        last = step == ITERS - 1

        def one_pass(carry, block):
            expo = block_expo(block, centroids, norms)
            row_scale = 1.0 / jnp.sum(expo * col_scale[None, :], axis=1)
            assign = expo * row_scale[:, None] * col_scale[None, :]
            mass = carry[0] + jnp.sum(expo * row_scale[:, None], axis=0)
            weight = carry[1] + jnp.sum(assign, axis=0)
            numer = carry[2]
            if last:
                low = assign.astype(jnp.bfloat16)
                numer = numer + lax.dot_general(low, block, (((0,), (0,)), ((), ())), preferred_element_type=jnp.float32)
            return (mass, weight, numer), row_scale

        init = (jnp.zeros((K,), jnp.float32), jnp.zeros((K,), jnp.float32), jnp.zeros((K, D), jnp.float32))
        (column_mass, weight, numer), scales = lax.scan(one_pass, init, blocks)
        if not last:
            col_scale = ratio / jnp.maximum(column_mass, 1.0)
    new_centroids = numer / jnp.maximum(weight, 1.0)[:, None]
    log_scale = jnp.log(scales.reshape(ROWS))
    return new_centroids, log_scale
```

```python
import functools
import math

import jax
import jax.numpy as jnp
from jax import lax
from jax.experimental import pallas as pl
from jax.experimental.pallas import tpu as pltpu
from jax.sharding import PartitionSpec as P

ITERS = 3
TAU = 0.05
LOG2E = math.log2(math.e)

NX, NY, NZ = 4, 4, 8
R = 2048
K = 2048
D = 256
HALF = K // 2
GROUP = HALF // NZ
SHARD = GROUP // NY
LANES = 128
CHUNKS = R // LANES
MESH = pl.DeviceIdType.MESH
NT = (((1,), (1,)), ((), ()))


def far_first(i):
    half = (i + 1) // 2
    return 4 + half * (1 - 2 * lax.rem(i, 2))


def kernel(
    ratio, p_ref, c_ref, new_ref, log_ref,
    expo, col_b, row_b, acc, norm_b, peak8, factor,
    dense, pre, own, colbuf, total, rowpart, xbuf,
    low, numer, corebuf, ybuf, zsrc, zbuf,
    pre_s, pre_r, col_s, col_r, post_s, post_r, x_s, x_r,
    core_s, core_r, y_s, y_r, z_s, z_r, agz_s, agz_r, agy_s, agy_r, agc_s, agc_r,
):
    x = lax.axis_index("cents")
    rows = lax.axis_index("rows")
    core = lax.rem(rows, 2)
    z = lax.rem(rows // 2, NZ)
    y = rows // (2 * NZ)
    other = 1 - core

    def dev(dx=0, dy=0, dz=0, flip=False):
        yy = lax.rem(y + dy, NY)
        zz = lax.rem(z + dz, NZ)
        cc = other if flip else core
        return {"rows": (yy * NZ + zz) * 2 + cc, "cents": lax.rem(x + dx, NX)}

    def copy(src, dst, send, recv, to):
        return pltpu.make_async_remote_copy(
            src_ref=src, dst_ref=dst, send_sem=send, recv_sem=recv, device_id=to, device_id_type=MESH
        )

    barrier = pltpu.get_barrier_semaphore()

    def greet(i, carry):
        dz = far_first(i)
        for dy in (2, 1, 3):
            pl.semaphore_signal(barrier, inc=1, device_id=dev(dy=dy, dz=dz), device_id_type=MESH)

        @pl.when(i < NZ - 1)
        def _():
            pl.semaphore_signal(barrier, inc=1, device_id=dev(dz=dz), device_id_type=MESH)

        return carry

    lax.fori_loop(0, NZ, greet, 0)
    for dx in (2, 1, 3):
        pl.semaphore_signal(barrier, inc=1, device_id=dev(dx=dx), device_id_type=MESH)
    pl.semaphore_signal(barrier, inc=1, device_id=dev(flip=True), device_id_type=MESH)

    def norms(q, carry):
        at = pl.ds(pl.multiple_of(q * 256, 256), 256)
        cent = c_ref[at, :].astype(jnp.float32)
        norm_b[at, :] = jnp.broadcast_to(
            jnp.sum(cent * cent, axis=1, keepdims=True) * (LOG2E / TAU), (256, LANES)
        )
        return carry

    lax.fori_loop(0, K // 256, norms, 0)

    def scores(b, carry):
        lanes = pl.ds(pl.multiple_of(b * 256, 256), 256)
        block = p_ref[lanes, :]

        def part(q, top):
            at = pl.ds(pl.multiple_of(q * 512, 512), 512)
            s = lax.dot_general(c_ref[at, :], block, NT, preferred_element_type=jnp.float32)
            bias = norm_b[at, :]
            t = s * (2.0 * LOG2E / TAU) - jnp.concatenate([bias, bias], axis=1)
            expo[at, lanes] = t
            return jnp.maximum(top, jnp.max(t.reshape(64, 8, 256), axis=0))

        top = lax.fori_loop(0, K // 512, part, jnp.full((8, 256), -jnp.inf, jnp.float32))
        top = jnp.max(top, axis=0, keepdims=True)
        peak8[:, lanes] = jnp.broadcast_to(top, (8, 256))
        return carry

    lax.fori_loop(0, R // 256, scores, 0)

    def exps(q, carry):
        at = pl.ds(pl.multiple_of(q * 8, 8), 8)
        for k in range(CHUNKS):
            lanes = slice(k * LANES, (k + 1) * LANES)
            expo[at, lanes] = jnp.exp2(expo[at, lanes] - peak8[:, lanes])
        return carry

    lax.fori_loop(0, K // 8, exps, 0, unroll=4)

    def to_dense(src8, dst):
        for g in range(CHUNKS):
            dst[g : g + 1, :] = src8[0:1, g * LANES : (g + 1) * LANES]

    def to_lanes(value, dst8):
        for g in range(CHUNKS):
            dst8[:, g * LANES : (g + 1) * LANES] = jnp.broadcast_to(value[g : g + 1, :], (8, LANES))

    to_dense(peak8, rowpart.at[0])
    pl.semaphore_wait(barrier, NY * NZ - 1 + NX - 1 + 1)

    def x_exchange(t):
        xbuf[t, x] = rowpart[t]

        def one(dx):
            return copy(rowpart.at[t], xbuf.at[t, x], x_s.at[t, dx - 1], x_r.at[t, dx - 1], dev(dx=dx))

        for dx in (2, 1, 3):
            one(dx).start()
        for dx in (1, 3, 2):
            one(dx).wait_recv()
        for dx in (1, 3, 2):
            one(dx).wait_send()

    x_exchange(0)
    peak = jnp.maximum(jnp.maximum(xbuf[0, 0], xbuf[0, 1]), jnp.maximum(xbuf[0, 2], xbuf[0, 3]))
    factor[...] = jnp.exp2(rowpart[0] - peak)
    to_lanes(factor[...], row_b)

    ones = jnp.ones((8, LANES), jnp.float32)

    def lane_sums(h, t):
        for g in range(NZ):
            at = pl.ds(pl.multiple_of(h * HALF + g * LANES, LANES), LANES)
            s = lax.dot_general(
                ones, acc[at, :], NT, preferred_element_type=jnp.float32, precision=lax.Precision.HIGHEST
            )
            dense[t, h, g : g + 1, :] = s[0:1, :]

    def col_pass(h):
        r = [row_b[:, k * LANES : (k + 1) * LANES] for k in range(CHUNKS)]

        def body(q, carry):
            at = pl.ds(pl.multiple_of(h * HALF + q * 8, 8), 8)
            terms = [expo[at, k * LANES : (k + 1) * LANES] * r[k] for k in range(CHUNKS)]
            while len(terms) > 1:
                terms = [a + b for a, b in zip(terms[::2], terms[1::2])]
            acc[at, :] = terms[0]
            return carry

        lax.fori_loop(0, HALF // 8, body, 0, unroll=4)

    def row_pass(h, carry):
        def body(q, carry):
            at = pl.ds(pl.multiple_of(h * HALF + q * 8, 8), 8)
            c = col_b[at, :]
            return tuple(carry[k] + expo[at, k * LANES : (k + 1) * LANES] * c for k in range(CHUNKS))

        return lax.fori_loop(0, HALF // 8, body, carry, unroll=4)

    def pre_copy(t):
        return copy(dense.at[t, other], pre.at[t], pre_s.at[t], pre_r.at[t], dev(flip=True))

    def post_copy(t):
        return copy(total.at[t, core], total.at[t, core], post_s.at[t], post_r.at[t], dev(flip=True))

    def col_copy(t, i, dy):
        k = i * NY + dy
        return copy(own.at[t], colbuf.at[t, k], col_s.at[t, k], col_r.at[t, k], dev(dy=dy, dz=far_first(i)))

    def each_peer(act):
        def body(i, carry):
            for dy in (2, 1, 3):
                act(i, dy)

            @pl.when(i < NZ - 1)
            def _():
                act(i, 0)

            return carry

        lax.fori_loop(0, NZ, body, 0)

    def col_send(t):
        pre_copy(t).wait_recv()
        own[t] = dense[t, core] + pre[t]
        each_peer(lambda i, dy: col_copy(t, i, dy).start())

    def col_finish(t):
        each_peer(lambda i, dy: col_copy(t, i, dy).wait_recv())
        terms = [colbuf[t, k] for k in range(NY * NZ) if k != NY * (NZ - 1)] + [own[t]]
        while len(terms) > 1:
            terms = [a + b for a, b in zip(terms[::2], terms[1::2])]
        total[t, core] = terms[0]
        each_peer(lambda i, dy: col_copy(t, i, dy).wait_send())
        pre_copy(t).wait_send()

    def scale_half(t, h):
        scale = ratio / jnp.maximum(total[t, h], 1.0)
        for g in range(NZ):
            at = pl.ds(pl.multiple_of(h * HALF + g * LANES, LANES), LANES)
            col_b[at, :] = jnp.broadcast_to(scale[g : g + 1, :], (LANES, LANES)).T

    def one_round(t, carry):
        col_pass(other)
        lane_sums(other, t)
        pre_copy(t).start()
        col_pass(core)
        lane_sums(core, t)
        col_send(t)
        col_finish(t)
        post_copy(t).start()
        scale_half(t, core)
        mass = row_pass(core, tuple(jnp.zeros((8, LANES), jnp.float32) for _ in range(CHUNKS)))
        post_copy(t).wait_recv()
        scale_half(t, other)
        mass = row_pass(other, mass)
        for g in range(CHUNKS):
            rowpart[t + 1, g : g + 1, :] = jnp.sum(mass[g], axis=0, keepdims=True)
        rowpart[t + 1] = rowpart[t + 1] * factor[...]
        x_exchange(t + 1)
        row_mass = (xbuf[t + 1, 0] + xbuf[t + 1, 1]) + (xbuf[t + 1, 2] + xbuf[t + 1, 3])
        log_ref[...] = -jnp.log(row_mass)
        to_lanes(factor[...] / row_mass, row_b)
        post_copy(t).wait_send()
        return carry

    lax.fori_loop(0, ITERS, one_round, 0)

    def core_copy(i):
        return copy(numer.at[i, 1], corebuf.at[i], core_s.at[i], core_r.at[i], dev(flip=True))

    def y_copy(i, dy):
        at = pl.ds(pl.multiple_of(lax.rem(y + dy, NY) * SHARD, SHARD), SHARD)
        return copy(numer.at[i, 0, at], ybuf.at[i, dy - 1], y_s.at[i, dy - 1], y_r.at[i, dy - 1], dev(dy=dy))

    def z_copy(i):
        return copy(zsrc.at[i], zbuf.at[i], z_s.at[i], z_r.at[i], dev(dz=far_first(i)))

    def group(i, carry):
        @pl.when(i < NZ)
        def _():
            to = lax.rem(z + far_first(i), NZ)
            for n, h in enumerate((core, other)):
                base = h * HALF + to * GROUP

                def body(q, carry):
                    at = pl.ds(pl.multiple_of(base + q * 16, 16), 16)
                    c = col_b[at, :]
                    terms = []
                    for k in range(CHUNKS):
                        lanes = slice(k * LANES, (k + 1) * LANES)
                        r = row_b[:, lanes]
                        w = expo[at, lanes] * jnp.concatenate([r, r], axis=0) * c
                        low[pl.ds(pl.multiple_of(n * GROUP + q * 16, 16), 16), lanes] = w.astype(jnp.bfloat16)
                        terms.append(w)
                    while len(terms) > 1:
                        terms = [a + b for a, b in zip(terms[::2], terms[1::2])]
                    acc[at, :] = terms[0]
                    return carry

                lax.fori_loop(0, GROUP // 16, body, 0, unroll=2)
            both = jnp.dot(low[...], p_ref[...], preferred_element_type=jnp.float32)
            numer[i, 0] = both[:GROUP]
            numer[i, 1] = both[GROUP:]
            core_copy(i).start()

        @pl.when(i >= 2)
        def _():
            j = i - 2
            core_copy(j).wait_recv()
            numer[j, 0] = numer[j, 0] + corebuf[j]
            for dy in (2, 1, 3):
                y_copy(j, dy).start()

        return carry

    lax.fori_loop(0, NZ + 2, group, 0)

    lane_sums(other, ITERS)
    pre_copy(ITERS).start()
    lane_sums(core, ITERS)
    col_send(ITERS)

    def z_step(i, carry):
        for dy in (1, 3, 2):
            y_copy(i, dy).wait_recv()
        at = pl.ds(pl.multiple_of(y * SHARD, SHARD), SHARD)
        zsrc[i] = (numer[i, 0, at] + ybuf[i, 0]) + (ybuf[i, 1] + ybuf[i, 2])

        @pl.when(i < NZ - 1)
        def _():
            z_copy(i).start()

        return carry

    lax.fori_loop(0, NZ, z_step, 0)

    col_finish(ITERS)
    weight = jnp.maximum(total[ITERS, core, pl.ds(z, 1), :], 1.0)
    norm_b[0:LANES, :] = jnp.broadcast_to(weight, (LANES, LANES)).T

    for i in range(NZ - 1):
        z_copy(i).wait_recv()
    numer_sum = zsrc[NZ - 1]
    for i in range(NZ - 1):
        numer_sum = numer_sum + zbuf[i]
    w = norm_b[pl.ds(pl.multiple_of(y * SHARD, SHARD), SHARD), :]

    def piece(zz, yy):
        return new_ref.at[pl.ds(pl.multiple_of(core * HALF + zz * GROUP + yy * SHARD, SHARD), SHARD)]

    mine = piece(z, y)
    mine[...] = numer_sum / jnp.concatenate([w, w], axis=1)

    def agz_copy(i):
        return copy(mine, mine, agz_s.at[i], agz_r.at[i], dev(dz=far_first(i)))

    def agy_copy(i, dy):
        part = piece(lax.rem(z + NZ - far_first(i), NZ), y)
        return copy(part, part, agy_s.at[i, dy - 1], agy_r.at[i, dy - 1], dev(dy=dy))

    def agc_copy(i):
        zz = lax.rem(z + NZ - far_first(i), NZ)
        part = new_ref.at[pl.ds(pl.multiple_of(core * HALF + zz * GROUP, GROUP), GROUP)]
        return copy(part, part, agc_s.at[i], agc_r.at[i], dev(flip=True))

    def gather_z(i, carry):
        agz_copy(i).start()
        return carry

    lax.fori_loop(0, NZ - 1, gather_z, 0)

    def gather_y(n, carry):
        i = NZ - 1 - n

        @pl.when(n > 0)
        def _():
            agz_copy(i).wait_recv()

        for dy in (2, 1, 3):
            agy_copy(i, dy).start()
        return carry

    lax.fori_loop(0, NZ, gather_y, 0)

    def gather_core(n, carry):
        i = NZ - 1 - n
        for dy in (1, 3, 2):
            agy_copy(i, dy).wait_recv()
        agc_copy(i).start()
        return carry

    lax.fori_loop(0, NZ, gather_core, 0)

    def finish(i, carry):
        agc_copy(i).wait_recv()
        agc_copy(i).wait_send()
        core_copy(i).wait_send()
        for dy in (1, 2, 3):
            y_copy(i, dy).wait_send()
            agy_copy(i, dy).wait_send()

        @pl.when(i < NZ - 1)
        def _():
            z_copy(i).wait_send()
            agz_copy(i).wait_send()

        return carry

    lax.fori_loop(0, NZ, finish, 0)


def local(patients, centroids):
    ratio = float(R * NY * NZ * 2) / float(K * NX)
    f32 = jnp.float32
    T = ITERS + 1
    dma = pltpu.SemaphoreType.DMA
    vm = pltpu.VMEM
    new, log = pl.pallas_call(
        functools.partial(kernel, ratio),
        out_shape=(jax.ShapeDtypeStruct((K, D), f32), jax.ShapeDtypeStruct((CHUNKS, LANES), f32)),
        in_specs=[pl.BlockSpec(memory_space=pltpu.VMEM)] * 2,
        out_specs=[pl.BlockSpec(memory_space=pltpu.VMEM)] * 2,
        scratch_shapes=[
            vm((K, R), f32), vm((K, LANES), f32), vm((8, R), f32), vm((K, LANES), f32), vm((K, LANES), f32),
            vm((8, R), f32), vm((CHUNKS, LANES), f32),
            vm((T, 2, NZ, LANES), f32), vm((T, NZ, LANES), f32), vm((T, NZ, LANES), f32),
            vm((T, NY * NZ, NZ, LANES), f32), vm((T, 2, NZ, LANES), f32),
            vm((T, CHUNKS, LANES), f32), vm((T, NX, CHUNKS, LANES), f32),
            vm((2 * GROUP, R), jnp.bfloat16), vm((NZ, 2, GROUP, D), f32), vm((NZ, GROUP, D), f32),
            vm((NZ, NY - 1, SHARD, D), f32), vm((NZ, SHARD, D), f32), vm((NZ - 1, SHARD, D), f32),
            dma((T,)), dma((T,)), dma((T, NY * NZ)), dma((T, NY * NZ)), dma((T,)), dma((T,)),
            dma((T, NX - 1)), dma((T, NX - 1)),
            dma((NZ,)), dma((NZ,)), dma((NZ, NY - 1)), dma((NZ, NY - 1)), dma((NZ,)), dma((NZ,)),
            dma((NZ,)), dma((NZ,)), dma((NZ, NY - 1)), dma((NZ, NY - 1)), dma((NZ,)), dma((NZ,)),
        ],
        compiler_params=pltpu.CompilerParams(
            collective_id=0, has_side_effects=True, vmem_limit_bytes=48 << 20
        ),
    )(patients, centroids)
    return new, log.reshape(R)


def solution(mesh):
    return jax.shard_map(
        local,
        mesh=mesh,
        in_specs=(P("rows", None), P("cents", None)),
        out_specs=(P("cents", None), P("rows")),
        check_vma=False,
    )
```

```python
import functools
import math

import jax
import jax.numpy as jnp
from jax import lax
from jax.experimental import pallas as pl
from jax.experimental.pallas import tpu as pltpu
from jax.sharding import PartitionSpec as P

ITERS = 3
TAU = 0.05
LOG2E = math.log2(math.e)

NX, NY, NZ = 4, 4, 8
R = 2048
K = 2048
D = 256
HALF = K // 2
GROUP = HALF // NZ
SHARD = GROUP // NY
LANES = 128
CHUNKS = R // LANES
MESH = pl.DeviceIdType.MESH
Y_LAG = 4
G_LAG = 4
NT = (((1,), (1,)), ((), ()))


def far_first(i):
    half = (i + 1) // 2
    return 4 + half * (1 - 2 * lax.rem(i, 2))


def kernel(
    ratio, p_hbm, c_hbm, new_ref, log_ref, p_ref, c_ref, t_even, t_odd, in_s,
    expo, col_b, row_b, acc, norm_b, peak8, factor,
    dense, pre, own, colbuf, total, rowpart, xbuf,
    low, numer, corebuf, relaybuf, ybuf, zsrc, zbuf,
    pre_s, pre_r, col_s, col_r, post_s, post_r, x_s, x_r,
    core_s, core_r, relay_s, relay_r, y_s, y_r, z_s, z_r, agz_s, agz_r, agy_s, agy_r, agf_s, agf_r, agc_s, agc_r,
):
    x = lax.axis_index("cents")
    rows = lax.axis_index("rows")
    core = lax.rem(rows, 2)
    z = lax.rem(rows // 2, NZ)
    y = rows // (2 * NZ)
    other = 1 - core

    def dev(dx=0, dy=0, dz=0, flip=False):
        yy = lax.rem(y + dy, NY)
        zz = lax.rem(z + dz, NZ)
        cc = other if flip else core
        return {"rows": (yy * NZ + zz) * 2 + cc, "cents": lax.rem(x + dx, NX)}

    def copy(src, dst, send, recv, to):
        return pltpu.make_async_remote_copy(
            src_ref=src, dst_ref=dst, send_sem=send, recv_sem=recv, device_id=to, device_id_type=MESH
        )

    fetch_c = pltpu.make_async_copy(c_hbm, c_ref, in_s.at[0])
    fetch_p = pltpu.make_async_copy(p_hbm, p_ref, in_s.at[1])
    fetch_c.start()
    fetch_p.start()

    barrier = pltpu.get_barrier_semaphore()

    def greet(i, carry):
        dz = far_first(i)
        for dy in (2, 1, 3):
            pl.semaphore_signal(barrier, inc=1, device_id=dev(dy=dy, dz=dz), device_id_type=MESH)

        @pl.when(i < NZ - 1)
        def _():
            pl.semaphore_signal(barrier, inc=1, device_id=dev(dz=dz), device_id_type=MESH)

        return carry

    lax.fori_loop(0, NZ, greet, 0)
    for dx in (2, 1, 3):
        pl.semaphore_signal(barrier, inc=1, device_id=dev(dx=dx), device_id_type=MESH)
    pl.semaphore_signal(barrier, inc=1, device_id=dev(flip=True), device_id_type=MESH)

    def norms(q, carry):
        at = pl.ds(pl.multiple_of(q * 256, 256), 256)
        cent = c_ref[at, :].astype(jnp.float32)
        norm_b[at, :] = jnp.broadcast_to(
            jnp.sum(cent * cent, axis=1, keepdims=True) * (LOG2E / TAU), (256, LANES)
        )
        return carry

    fetch_c.wait()
    lax.fori_loop(0, K // 256, norms, 0)
    fetch_p.wait()

    def block_lanes(b):
        return pl.ds(pl.multiple_of(b * 256, 256), 256)

    def score_part(q, b, buf):
        at = slice(q * 512, (q + 1) * 512)
        s = lax.dot_general(c_ref[at, :], p_ref[block_lanes(b), :], NT, preferred_element_type=jnp.float32)
        bias = norm_b[at, :]
        t = s * (2.0 * LOG2E / TAU) - jnp.concatenate([bias, bias], axis=1)
        buf[at, :] = t
        return jnp.max(t.reshape(64, 8, 256), axis=0)

    def exp_part(q, b, buf, top):
        at = slice(q * 512, (q + 1) * 512)
        expo[at, block_lanes(b)] = jnp.exp2(buf[at, :] - top)

    def set_peak(b, tops):
        top = jnp.max(jnp.maximum(jnp.maximum(tops[0], tops[1]), jnp.maximum(tops[2], tops[3])), axis=0, keepdims=True)
        peak8[:, block_lanes(b)] = jnp.broadcast_to(top, (8, 256))

    def step(b, buf, last):
        top = peak8[0:1, block_lanes(b - 1)]
        tops = []
        for q in range(4):
            tops.append(score_part(q, b, buf))
            exp_part(q, b - 1, last, top)
        set_peak(b, tops)

    set_peak(0, [score_part(q, 0, t_even) for q in range(4)])

    def pair(m, carry):
        step(2 * m + 1, t_odd, t_even)
        step(2 * m + 2, t_even, t_odd)
        return carry

    lax.fori_loop(0, R // 512 - 1, pair, 0)
    step(R // 256 - 1, t_odd, t_even)
    for q in range(4):
        exp_part(q, R // 256 - 1, t_odd, peak8[0:1, R - 256 :])

    def to_dense(src8, dst):
        for g in range(CHUNKS):
            dst[g : g + 1, :] = src8[0:1, g * LANES : (g + 1) * LANES]

    def to_lanes(value, dst8):
        for g in range(CHUNKS):
            dst8[:, g * LANES : (g + 1) * LANES] = jnp.broadcast_to(value[g : g + 1, :], (8, LANES))

    to_dense(peak8, rowpart.at[0])
    pl.semaphore_wait(barrier, NY * NZ - 1 + NX - 1 + 1)

    def x_exchange(t):
        xbuf[t, x] = rowpart[t]

        def one(dx):
            return copy(rowpart.at[t], xbuf.at[t, x], x_s.at[t, dx - 1], x_r.at[t, dx - 1], dev(dx=dx))

        for dx in (2, 1, 3):
            one(dx).start()
        for dx in (1, 3, 2):
            one(dx).wait_recv()
        for dx in (1, 3, 2):
            one(dx).wait_send()

    x_exchange(0)
    peak = jnp.maximum(jnp.maximum(xbuf[0, 0], xbuf[0, 1]), jnp.maximum(xbuf[0, 2], xbuf[0, 3]))
    factor[...] = jnp.exp2(rowpart[0] - peak)
    to_lanes(factor[...], row_b)

    ones = jnp.ones((8, LANES), jnp.float32)

    def lane_sums(h, t):
        for g in range(NZ):
            at = pl.ds(pl.multiple_of(h * HALF + g * LANES, LANES), LANES)
            s = lax.dot_general(
                ones, acc[at, :], NT, preferred_element_type=jnp.float32, precision=lax.Precision.HIGHEST
            )
            dense[t, h, g : g + 1, :] = s[0:1, :]

    def col_pass(h):
        r = [row_b[:, k * LANES : (k + 1) * LANES] for k in range(CHUNKS)]

        def body(q, carry):
            at = pl.ds(pl.multiple_of(h * HALF + q * 8, 8), 8)
            terms = [expo[at, k * LANES : (k + 1) * LANES] * r[k] for k in range(CHUNKS)]
            while len(terms) > 1:
                terms = [a + b for a, b in zip(terms[::2], terms[1::2])]
            acc[at, :] = terms[0]
            return carry

        lax.fori_loop(0, HALF // 8, body, 0, unroll=4)

    def row_pass(h, carry):
        def body(q, carry):
            at = pl.ds(pl.multiple_of(h * HALF + q * 8, 8), 8)
            c = col_b[at, :]
            return tuple(carry[k] + expo[at, k * LANES : (k + 1) * LANES] * c for k in range(CHUNKS))

        return lax.fori_loop(0, HALF // 8, body, carry, unroll=4)

    def pre_copy(t):
        return copy(dense.at[t, other], pre.at[t], pre_s.at[t], pre_r.at[t], dev(flip=True))

    def post_copy(t):
        return copy(total.at[t, core], total.at[t, core], post_s.at[t], post_r.at[t], dev(flip=True))

    def col_copy(t, i, dy):
        k = i * NY + dy
        return copy(own.at[t], colbuf.at[t, k], col_s.at[t, k], col_r.at[t, k], dev(dy=dy, dz=far_first(i)))

    def each_peer(act):
        def body(i, carry):
            for dy in (2, 1, 3):
                act(i, dy)

            @pl.when(i < NZ - 1)
            def _():
                act(i, 0)

            return carry

        lax.fori_loop(0, NZ, body, 0)

    def col_send(t):
        pre_copy(t).wait_recv()
        own[t] = dense[t, core] + pre[t]
        each_peer(lambda i, dy: col_copy(t, i, dy).start())

    def col_finish(t):
        each_peer(lambda i, dy: col_copy(t, i, dy).wait_recv())
        terms = [colbuf[t, k] for k in range(NY * NZ) if k != NY * (NZ - 1)] + [own[t]]
        while len(terms) > 1:
            terms = [a + b for a, b in zip(terms[::2], terms[1::2])]
        total[t, core] = terms[0]
        each_peer(lambda i, dy: col_copy(t, i, dy).wait_send())
        pre_copy(t).wait_send()

    def scale_half(t, h):
        scale = ratio / jnp.maximum(total[t, h], 1.0)
        for g in range(NZ):
            at = pl.ds(pl.multiple_of(h * HALF + g * LANES, LANES), LANES)
            col_b[at, :] = jnp.broadcast_to(scale[g : g + 1, :], (LANES, LANES)).T

    def one_round(t, carry):
        col_pass(other)
        lane_sums(other, t)
        pre_copy(t).start()
        col_pass(core)
        lane_sums(core, t)
        col_send(t)
        col_finish(t)
        post_copy(t).start()
        scale_half(t, core)
        mass = row_pass(core, tuple(jnp.zeros((8, LANES), jnp.float32) for _ in range(CHUNKS)))
        post_copy(t).wait_recv()
        scale_half(t, other)
        mass = row_pass(other, mass)
        for g in range(CHUNKS):
            rowpart[t + 1, g : g + 1, :] = jnp.sum(mass[g], axis=0, keepdims=True)
        rowpart[t + 1] = rowpart[t + 1] * factor[...]
        x_exchange(t + 1)
        row_mass = (xbuf[t + 1, 0] + xbuf[t + 1, 1]) + (xbuf[t + 1, 2] + xbuf[t + 1, 3])
        log_ref[...] = -jnp.log(row_mass)
        to_lanes(factor[...] / row_mass, row_b)
        post_copy(t).wait_send()
        return carry

    lax.fori_loop(0, ITERS, one_round, 0)

    def core_copy(i):
        return copy(numer.at[i, 1], corebuf.at[i], core_s.at[i], core_r.at[i], dev(flip=True))

    near, back = 1 + 2 * core, 3 - 2 * core

    def part_of(i, dy):
        return numer.at[i, 0, pl.ds(pl.multiple_of(lax.rem(y + dy, NY) * SHARD, SHARD), SHARD)]

    def relay_copy(i):
        return copy(part_of(i, 2), relaybuf.at[i], relay_s.at[i], relay_r.at[i], dev(dy=near))

    def y_copy(i, n):
        dy = (near, back)[n]
        return copy(part_of(i, dy), ybuf.at[i, n], y_s.at[i, n], y_r.at[i, n], dev(dy=dy))

    def z_copy(i):
        return copy(zsrc.at[i], zbuf.at[i], z_s.at[i], z_r.at[i], dev(dz=far_first(i)))

    def group(i, carry):
        @pl.when(i < NZ)
        def _():
            to = lax.rem(z + far_first(i), NZ)
            for n, h in enumerate((core, other)):
                base = h * HALF + to * GROUP

                def body(q, carry):
                    at = pl.ds(pl.multiple_of(base + q * 16, 16), 16)
                    c = col_b[at, :]
                    terms = []
                    for k in range(CHUNKS):
                        lanes = slice(k * LANES, (k + 1) * LANES)
                        r = row_b[:, lanes]
                        w = expo[at, lanes] * jnp.concatenate([r, r], axis=0) * c
                        low[pl.ds(pl.multiple_of(n * GROUP + q * 16, 16), 16), lanes] = w.astype(jnp.bfloat16)
                        terms.append(w)
                    while len(terms) > 1:
                        terms = [a + b for a, b in zip(terms[::2], terms[1::2])]
                    acc[at, :] = terms[0]
                    return carry

                lax.fori_loop(0, GROUP // 16, body, 0, unroll=2)
            both = jnp.dot(low[...], p_ref[...], preferred_element_type=jnp.float32)
            numer[i, 0] = both[:GROUP]
            numer[i, 1] = both[GROUP:]
            core_copy(i).start()

        @pl.when(i >= 2)
        def _():
            j = i - 2
            core_copy(j).wait_recv()
            numer[j, 0] = numer[j, 0] + corebuf[j]
            relay_copy(j).start()
            y_copy(j, 1).start()

        return carry

    lax.fori_loop(0, NZ + 2, group, 0)

    lane_sums(other, ITERS)
    pre_copy(ITERS).start()
    lane_sums(core, ITERS)
    col_send(ITERS)

    def relay(i):
        relay_copy(i).wait_recv()
        part = part_of(i, near)
        part[...] = part[...] + relaybuf[i]
        y_copy(i, 0).start()

    def z_step(i):
        y_copy(i, 1).wait_recv()
        y_copy(i, 0).wait_recv()
        zsrc[i] = part_of(i, 0)[...] + (ybuf[i, 0] + ybuf[i, 1])

        @pl.when(i < NZ - 1)
        def _():
            z_copy(i).start()

    def scatter(n, carry):
        @pl.when(n < NZ)
        def _():
            relay(n)

        @pl.when(n >= Y_LAG)
        def _():
            z_step(n - Y_LAG)

        return carry

    lax.fori_loop(0, NZ + Y_LAG, scatter, 0)

    col_finish(ITERS)
    weight = jnp.maximum(total[ITERS, core, pl.ds(z, 1), :], 1.0)
    norm_b[0:LANES, :] = jnp.broadcast_to(weight, (LANES, LANES)).T

    for i in range(NZ - 1):
        z_copy(i).wait_recv()
    numer_sum = zsrc[NZ - 1]
    for i in range(NZ - 1):
        numer_sum = numer_sum + zbuf[i]
    w = norm_b[pl.ds(pl.multiple_of(y * SHARD, SHARD), SHARD), :]

    def piece(zz, yy):
        return new_ref.at[pl.ds(pl.multiple_of(core * HALF + zz * GROUP + yy * SHARD, SHARD), SHARD)]

    mine = piece(z, y)
    mine[...] = numer_sum / jnp.concatenate([w, w], axis=1)

    def agz_copy(i):
        return copy(mine, mine, agz_s.at[i], agz_r.at[i], dev(dz=far_first(i)))

    def from_z(i):
        return lax.rem(z + NZ - far_first(i), NZ)

    def agy_copy(i, n):
        part = piece(from_z(i), y)
        return copy(part, part, agy_s.at[i, n], agy_r.at[i, n], dev(dy=(near, back)[n]))

    def agf_copy(i):
        part = piece(from_z(i), lax.rem(y + back, NY))
        return copy(part, part, agf_s.at[i], agf_r.at[i], dev(dy=near))

    def agc_copy(i):
        zz = from_z(i)
        part = new_ref.at[pl.ds(pl.multiple_of(core * HALF + zz * GROUP, GROUP), GROUP)]
        return copy(part, part, agc_s.at[i], agc_r.at[i], dev(flip=True))

    def gather_z(i, carry):
        agz_copy(i).start()
        return carry

    lax.fori_loop(0, NZ - 1, gather_z, 0)

    def gather(n, carry):
        @pl.when(n < NZ)
        def _():
            i = NZ - 1 - n

            @pl.when(n > 0)
            def _():
                agz_copy(i).wait_recv()

            agy_copy(i, 0).start()
            agy_copy(i, 1).start()

        @pl.when((n >= G_LAG) & (n < NZ + G_LAG))
        def _():
            i = NZ - 1 - (n - G_LAG)
            agy_copy(i, 0).wait_recv()
            agf_copy(i).start()

        @pl.when(n >= 2 * G_LAG)
        def _():
            i = NZ - 1 - (n - 2 * G_LAG)
            agy_copy(i, 1).wait_recv()
            agf_copy(i).wait_recv()
            agc_copy(i).start()

        return carry

    lax.fori_loop(0, NZ + 2 * G_LAG, gather, 0)

    def finish(i, carry):
        agc_copy(i).wait_recv()
        agc_copy(i).wait_send()
        core_copy(i).wait_send()
        relay_copy(i).wait_send()
        agf_copy(i).wait_send()
        for n in range(2):
            y_copy(i, n).wait_send()
            agy_copy(i, n).wait_send()

        @pl.when(i < NZ - 1)
        def _():
            z_copy(i).wait_send()
            agz_copy(i).wait_send()

        return carry

    lax.fori_loop(0, NZ, finish, 0)


def local(patients, centroids):
    ratio = float(R * NY * NZ * 2) / float(K * NX)
    f32 = jnp.float32
    T = ITERS + 1
    dma = pltpu.SemaphoreType.DMA
    vm = pltpu.VMEM
    new, log = pl.pallas_call(
        functools.partial(kernel, ratio),
        out_shape=(jax.ShapeDtypeStruct((K, D), f32), jax.ShapeDtypeStruct((CHUNKS, LANES), f32)),
        in_specs=[pl.BlockSpec(memory_space=pltpu.HBM)] * 2,
        out_specs=[pl.BlockSpec(memory_space=pltpu.VMEM)] * 2,
        scratch_shapes=[
            vm((R, D), jnp.bfloat16), vm((K, D), jnp.bfloat16), vm((K, 256), f32), vm((K, 256), f32), dma((2,)),
            vm((K, R), f32), vm((K, LANES), f32), vm((8, R), f32), vm((K, LANES), f32), vm((K, LANES), f32),
            vm((8, R), f32), vm((CHUNKS, LANES), f32),
            vm((T, 2, NZ, LANES), f32), vm((T, NZ, LANES), f32), vm((T, NZ, LANES), f32),
            vm((T, NY * NZ, NZ, LANES), f32), vm((T, 2, NZ, LANES), f32),
            vm((T, CHUNKS, LANES), f32), vm((T, NX, CHUNKS, LANES), f32),
            vm((2 * GROUP, R), jnp.bfloat16), vm((NZ, 2, GROUP, D), f32), vm((NZ, GROUP, D), f32),
            vm((NZ, SHARD, D), f32), vm((NZ, 2, SHARD, D), f32), vm((NZ, SHARD, D), f32), vm((NZ - 1, SHARD, D), f32),
            dma((T,)), dma((T,)), dma((T, NY * NZ)), dma((T, NY * NZ)), dma((T,)), dma((T,)),
            dma((T, NX - 1)), dma((T, NX - 1)),
            dma((NZ,)), dma((NZ,)), dma((NZ,)), dma((NZ,)), dma((NZ, 2)), dma((NZ, 2)), dma((NZ,)), dma((NZ,)),
            dma((NZ,)), dma((NZ,)), dma((NZ, 2)), dma((NZ, 2)), dma((NZ,)), dma((NZ,)), dma((NZ,)), dma((NZ,)),
        ],
        compiler_params=pltpu.CompilerParams(
            collective_id=0, has_side_effects=True, vmem_limit_bytes=48 << 20
        ),
    )(patients, centroids)
    return new, log.reshape(R)


def solution(mesh):
    return jax.shard_map(
        local,
        mesh=mesh,
        in_specs=(P("rows", None), P("cents", None)),
        out_specs=(P("cents", None), P("rows")),
        check_vma=False,
    )
```

```python
import functools
import math

import jax
import jax.numpy as jnp
from jax import lax
from jax.experimental import pallas as pl
from jax.experimental.pallas import tpu as pltpu
from jax.sharding import PartitionSpec as P

ITERS = 3
TAU = 0.05
LOG2E = math.log2(math.e)

NX, NY, NZ = 4, 4, 8
R = 2048
K = 2048
D = 256
HALF = K // 2
GROUP = HALF // NZ
SHARD = GROUP // NY
LANES = 128
CHUNKS = R // LANES
MESH = pl.DeviceIdType.MESH
Y_LAG = 7
G_LAG = 4
NT = (((1,), (1,)), ((), ()))


def far_first(i):
    half = (i + 1) // 2
    return 4 + half * (1 - 2 * lax.rem(i, 2))


def kernel(
    ratio, p_hbm, c_hbm, new_ref, log_ref, p_ref, c_ref, t_even, t_odd, in_s,
    expo, col_b, row_b, acc, norm_b, peak8, factor,
    dense, pre, own, colbuf, total, rowpart, xbuf,
    low, numer, corebuf, ybuf, zsrc, zbuf,
    pre_s, pre_r, col_s, col_r, post_s, post_r, x_s, x_r,
    core_s, core_r, y_s, y_r, z_s, z_r, agz_s, agz_r, agy_s, agy_r, agc_s, agc_r,
):
    x = lax.axis_index("cents")
    rows = lax.axis_index("rows")
    core = lax.rem(rows, 2)
    z = lax.rem(rows // 2, NZ)
    y = rows // (2 * NZ)
    other = 1 - core

    def dev(dx=0, dy=0, dz=0, flip=False):
        yy = lax.rem(y + dy, NY)
        zz = lax.rem(z + dz, NZ)
        cc = other if flip else core
        return {"rows": (yy * NZ + zz) * 2 + cc, "cents": lax.rem(x + dx, NX)}

    def copy(src, dst, send, recv, to):
        return pltpu.make_async_remote_copy(
            src_ref=src, dst_ref=dst, send_sem=send, recv_sem=recv, device_id=to, device_id_type=MESH
        )

    fetch_c = pltpu.make_async_copy(c_hbm, c_ref, in_s.at[0])
    fetch_p = pltpu.make_async_copy(p_hbm, p_ref, in_s.at[1])
    fetch_c.start()
    fetch_p.start()

    barrier = pltpu.get_barrier_semaphore()

    def greet(i, carry):
        dz = far_first(i)
        for dy in (2, 1, 3):
            pl.semaphore_signal(barrier, inc=1, device_id=dev(dy=dy, dz=dz), device_id_type=MESH)

        @pl.when(i < NZ - 1)
        def _():
            pl.semaphore_signal(barrier, inc=1, device_id=dev(dz=dz), device_id_type=MESH)

        return carry

    lax.fori_loop(0, NZ, greet, 0)
    for dx in (2, 1, 3):
        pl.semaphore_signal(barrier, inc=1, device_id=dev(dx=dx), device_id_type=MESH)
    pl.semaphore_signal(barrier, inc=1, device_id=dev(flip=True), device_id_type=MESH)

    def norms(q, carry):
        at = pl.ds(pl.multiple_of(q * 256, 256), 256)
        cent = c_ref[at, :].astype(jnp.float32)
        norm_b[at, :] = jnp.broadcast_to(
            jnp.sum(cent * cent, axis=1, keepdims=True) * (LOG2E / TAU), (256, LANES)
        )
        return carry

    fetch_c.wait()
    lax.fori_loop(0, K // 256, norms, 0)
    fetch_p.wait()

    def block_lanes(b):
        return pl.ds(pl.multiple_of(b * 256, 256), 256)

    def score_part(q, b, buf):
        at = slice(q * 512, (q + 1) * 512)
        s = lax.dot_general(c_ref[at, :], p_ref[block_lanes(b), :], NT, preferred_element_type=jnp.float32)
        bias = norm_b[at, :]
        t = s * (2.0 * LOG2E / TAU) - jnp.concatenate([bias, bias], axis=1)
        buf[at, :] = t
        return jnp.max(t.reshape(64, 8, 256), axis=0)

    def exp_part(q, b, buf, top):
        at = slice(q * 512, (q + 1) * 512)
        expo[at, block_lanes(b)] = jnp.exp2(buf[at, :] - top)

    def set_peak(b, tops):
        top = jnp.max(jnp.maximum(jnp.maximum(tops[0], tops[1]), jnp.maximum(tops[2], tops[3])), axis=0, keepdims=True)
        peak8[:, block_lanes(b)] = jnp.broadcast_to(top, (8, 256))

    def step(b, buf, last):
        top = peak8[0:1, block_lanes(b - 1)]
        tops = []
        for q in range(4):
            tops.append(score_part(q, b, buf))
            exp_part(q, b - 1, last, top)
        set_peak(b, tops)

    set_peak(0, [score_part(q, 0, t_even) for q in range(4)])

    def pair(m, carry):
        step(2 * m + 1, t_odd, t_even)
        step(2 * m + 2, t_even, t_odd)
        return carry

    lax.fori_loop(0, R // 512 - 1, pair, 0)
    step(R // 256 - 1, t_odd, t_even)
    for q in range(4):
        exp_part(q, R // 256 - 1, t_odd, peak8[0:1, R - 256 :])

    def to_dense(src8, dst):
        for g in range(CHUNKS):
            dst[g : g + 1, :] = src8[0:1, g * LANES : (g + 1) * LANES]

    def to_lanes(value, dst8):
        for g in range(CHUNKS):
            dst8[:, g * LANES : (g + 1) * LANES] = jnp.broadcast_to(value[g : g + 1, :], (8, LANES))

    to_dense(peak8, rowpart.at[0])
    pl.semaphore_wait(barrier, NY * NZ - 1 + NX - 1 + 1)

    def x_exchange(t):
        xbuf[t, x] = rowpart[t]

        def one(dx):
            return copy(rowpart.at[t], xbuf.at[t, x], x_s.at[t, dx - 1], x_r.at[t, dx - 1], dev(dx=dx))

        for dx in (2, 1, 3):
            one(dx).start()
        for dx in (1, 3, 2):
            one(dx).wait_recv()
        for dx in (1, 3, 2):
            one(dx).wait_send()

    x_exchange(0)
    peak = jnp.maximum(jnp.maximum(xbuf[0, 0], xbuf[0, 1]), jnp.maximum(xbuf[0, 2], xbuf[0, 3]))
    factor[...] = jnp.exp2(rowpart[0] - peak)
    to_lanes(factor[...], row_b)

    ones = jnp.ones((8, LANES), jnp.float32)

    def lane_sums(h, t):
        for g in range(NZ):
            at = pl.ds(pl.multiple_of(h * HALF + g * LANES, LANES), LANES)
            s = lax.dot_general(
                ones, acc[at, :], NT, preferred_element_type=jnp.float32, precision=lax.Precision.HIGHEST
            )
            dense[t, h, g : g + 1, :] = s[0:1, :]

    def col_pass(h):
        r = [row_b[:, k * LANES : (k + 1) * LANES] for k in range(CHUNKS)]

        def body(q, carry):
            at = pl.ds(pl.multiple_of(h * HALF + q * 8, 8), 8)
            terms = [expo[at, k * LANES : (k + 1) * LANES] * r[k] for k in range(CHUNKS)]
            while len(terms) > 1:
                terms = [a + b for a, b in zip(terms[::2], terms[1::2])]
            acc[at, :] = terms[0]
            return carry

        lax.fori_loop(0, HALF // 8, body, 0, unroll=4)

    def row_pass(h, carry):
        def body(q, carry):
            at = pl.ds(pl.multiple_of(h * HALF + q * 8, 8), 8)
            c = col_b[at, :]
            return tuple(carry[k] + expo[at, k * LANES : (k + 1) * LANES] * c for k in range(CHUNKS))

        return lax.fori_loop(0, HALF // 8, body, carry, unroll=4)

    def pre_copy(t):
        return copy(dense.at[t, other], pre.at[t], pre_s.at[t], pre_r.at[t], dev(flip=True))

    def post_copy(t):
        return copy(total.at[t, core], total.at[t, core], post_s.at[t], post_r.at[t], dev(flip=True))

    def col_copy(t, i, dy):
        k = i * NY + dy
        return copy(own.at[t], colbuf.at[t, k], col_s.at[t, k], col_r.at[t, k], dev(dy=dy, dz=far_first(i)))

    def each_peer(act):
        def body(i, carry):
            for dy in (2, 1, 3):
                act(i, dy)

            @pl.when(i < NZ - 1)
            def _():
                act(i, 0)

            return carry

        lax.fori_loop(0, NZ, body, 0)

    def col_send(t):
        pre_copy(t).wait_recv()
        own[t] = dense[t, core] + pre[t]
        each_peer(lambda i, dy: col_copy(t, i, dy).start())

    def col_finish(t):
        each_peer(lambda i, dy: col_copy(t, i, dy).wait_recv())
        terms = [colbuf[t, k] for k in range(NY * NZ) if k != NY * (NZ - 1)] + [own[t]]
        while len(terms) > 1:
            terms = [a + b for a, b in zip(terms[::2], terms[1::2])]
        total[t, core] = terms[0]
        each_peer(lambda i, dy: col_copy(t, i, dy).wait_send())
        pre_copy(t).wait_send()

    def scale_half(t, h):
        scale = ratio / jnp.maximum(total[t, h], 1.0)
        for g in range(NZ):
            at = pl.ds(pl.multiple_of(h * HALF + g * LANES, LANES), LANES)
            col_b[at, :] = jnp.broadcast_to(scale[g : g + 1, :], (LANES, LANES)).T

    def one_round(t, carry):
        col_pass(other)
        lane_sums(other, t)
        pre_copy(t).start()
        col_pass(core)
        lane_sums(core, t)
        col_send(t)
        col_finish(t)
        post_copy(t).start()
        scale_half(t, core)
        mass = row_pass(core, tuple(jnp.zeros((8, LANES), jnp.float32) for _ in range(CHUNKS)))
        post_copy(t).wait_recv()
        scale_half(t, other)
        mass = row_pass(other, mass)
        for g in range(CHUNKS):
            rowpart[t + 1, g : g + 1, :] = jnp.sum(mass[g], axis=0, keepdims=True)
        rowpart[t + 1] = rowpart[t + 1] * factor[...]
        x_exchange(t + 1)
        row_mass = (xbuf[t + 1, 0] + xbuf[t + 1, 1]) + (xbuf[t + 1, 2] + xbuf[t + 1, 3])
        log_ref[...] = -jnp.log(row_mass)
        to_lanes(factor[...] / row_mass, row_b)
        post_copy(t).wait_send()
        return carry

    lax.fori_loop(0, ITERS, one_round, 0)

    def core_copy(i):
        return copy(numer.at[i, 1], corebuf.at[i], core_s.at[i], core_r.at[i], dev(flip=True))

    def part_of(i, dy):
        return numer.at[i, 0, pl.ds(pl.multiple_of(lax.rem(y + dy, NY) * SHARD, SHARD), SHARD)]

    def y_copy(i, dy):
        return copy(part_of(i, dy), ybuf.at[i, dy - 1], y_s.at[i, dy - 1], y_r.at[i, dy - 1], dev(dy=dy))

    def z_copy(i):
        return copy(zsrc.at[i], zbuf.at[i], z_s.at[i], z_r.at[i], dev(dz=far_first(i)))

    def z_step(i):
        for dy in (1, 3, 2):
            y_copy(i, dy).wait_recv()
        zsrc[i] = (part_of(i, 0)[...] + ybuf[i, 0]) + (ybuf[i, 1] + ybuf[i, 2])

        @pl.when(i < NZ - 1)
        def _():
            z_copy(i).start()

    def group(i, carry):
        @pl.when(i < NZ)
        def _():
            to = lax.rem(z + far_first(i), NZ)
            for n, h in enumerate((core, other)):
                base = h * HALF + to * GROUP

                def body(q, carry):
                    at = pl.ds(pl.multiple_of(base + q * 16, 16), 16)
                    c = col_b[at, :]
                    terms = []
                    for k in range(CHUNKS):
                        lanes = slice(k * LANES, (k + 1) * LANES)
                        r = row_b[:, lanes]
                        w = expo[at, lanes] * jnp.concatenate([r, r], axis=0) * c
                        low[pl.ds(pl.multiple_of(n * GROUP + q * 16, 16), 16), lanes] = w.astype(jnp.bfloat16)
                        terms.append(w)
                    while len(terms) > 1:
                        terms = [a + b for a, b in zip(terms[::2], terms[1::2])]
                    acc[at, :] = terms[0]
                    return carry

                lax.fori_loop(0, GROUP // 16, body, 0, unroll=2)
            both = jnp.dot(low[...], p_ref[...], preferred_element_type=jnp.float32)
            numer[i, 0] = both[:GROUP]
            numer[i, 1] = both[GROUP:]
            core_copy(i).start()

        @pl.when(i >= 2)
        def _():
            j = i - 2
            core_copy(j).wait_recv()
            numer[j, 0] = numer[j, 0] + corebuf[j]
            for dy in (2, 1, 3):
                y_copy(j, dy).start()

        @pl.when(i >= Y_LAG)
        def _():
            z_step(i - Y_LAG)

        return carry

    lax.fori_loop(0, NZ + 2, group, 0)

    lane_sums(other, ITERS)
    pre_copy(ITERS).start()
    lane_sums(core, ITERS)
    col_send(ITERS)

    def scatter(i, carry):
        z_step(i)
        return carry

    lax.fori_loop(NZ + 2 - Y_LAG, NZ, scatter, 0)

    col_finish(ITERS)
    weight = jnp.maximum(total[ITERS, core, pl.ds(z, 1), :], 1.0)
    norm_b[0:LANES, :] = jnp.broadcast_to(weight, (LANES, LANES)).T

    for i in range(NZ - 1):
        z_copy(i).wait_recv()
    numer_sum = zsrc[NZ - 1]
    for i in range(NZ - 1):
        numer_sum = numer_sum + zbuf[i]
    w = norm_b[pl.ds(pl.multiple_of(y * SHARD, SHARD), SHARD), :]

    def piece(zz, yy):
        return new_ref.at[pl.ds(pl.multiple_of(core * HALF + zz * GROUP + yy * SHARD, SHARD), SHARD)]

    mine = piece(z, y)
    mine[...] = numer_sum / jnp.concatenate([w, w], axis=1)

    def agz_copy(i):
        return copy(mine, mine, agz_s.at[i], agz_r.at[i], dev(dz=far_first(i)))

    def from_z(i):
        return lax.rem(z + NZ - far_first(i), NZ)

    def agy_copy(i, dy):
        part = piece(from_z(i), y)
        return copy(part, part, agy_s.at[i, dy - 1], agy_r.at[i, dy - 1], dev(dy=dy))

    def agc_copy(i):
        zz = from_z(i)
        part = new_ref.at[pl.ds(pl.multiple_of(core * HALF + zz * GROUP, GROUP), GROUP)]
        return copy(part, part, agc_s.at[i], agc_r.at[i], dev(flip=True))

    def gather_z(i, carry):
        agz_copy(i).start()
        return carry

    gather_z(0, 0)
    lax.fori_loop(0, NZ - 2, lambda n, carry: gather_z(NZ - 2 - n, carry), 0)

    def gather(n, carry):
        @pl.when(n < NZ)
        def _():
            i = NZ - 1 - n

            @pl.when(n > 0)
            def _():
                agz_copy(i).wait_recv()

            for dy in (2, 1, 3):
                agy_copy(i, dy).start()

        @pl.when(n >= G_LAG)
        def _():
            i = NZ - 1 - (n - G_LAG)
            for dy in (1, 3, 2):
                agy_copy(i, dy).wait_recv()
            agc_copy(i).start()

        return carry

    lax.fori_loop(0, NZ + G_LAG, gather, 0)

    def finish(i, carry):
        agc_copy(i).wait_recv()
        agc_copy(i).wait_send()
        core_copy(i).wait_send()
        for dy in (1, 2, 3):
            y_copy(i, dy).wait_send()
            agy_copy(i, dy).wait_send()

        @pl.when(i < NZ - 1)
        def _():
            z_copy(i).wait_send()
            agz_copy(i).wait_send()

        return carry

    lax.fori_loop(0, NZ, finish, 0)


def local(patients, centroids):
    ratio = float(R * NY * NZ * 2) / float(K * NX)
    f32 = jnp.float32
    T = ITERS + 1
    dma = pltpu.SemaphoreType.DMA
    vm = pltpu.VMEM
    new, log = pl.pallas_call(
        functools.partial(kernel, ratio),
        out_shape=(jax.ShapeDtypeStruct((K, D), f32), jax.ShapeDtypeStruct((CHUNKS, LANES), f32)),
        in_specs=[pl.BlockSpec(memory_space=pltpu.HBM)] * 2,
        out_specs=[pl.BlockSpec(memory_space=pltpu.VMEM)] * 2,
        scratch_shapes=[
            vm((R, D), jnp.bfloat16), vm((K, D), jnp.bfloat16), vm((K, 256), f32), vm((K, 256), f32), dma((2,)),
            vm((K, R), f32), vm((K, LANES), f32), vm((8, R), f32), vm((K, LANES), f32), vm((K, LANES), f32),
            vm((8, R), f32), vm((CHUNKS, LANES), f32),
            vm((T, 2, NZ, LANES), f32), vm((T, NZ, LANES), f32), vm((T, NZ, LANES), f32),
            vm((T, NY * NZ, NZ, LANES), f32), vm((T, 2, NZ, LANES), f32),
            vm((T, CHUNKS, LANES), f32), vm((T, NX, CHUNKS, LANES), f32),
            vm((2 * GROUP, R), jnp.bfloat16), vm((NZ, 2, GROUP, D), f32), vm((NZ, GROUP, D), f32),
            vm((NZ, NY - 1, SHARD, D), f32), vm((NZ, SHARD, D), f32), vm((NZ - 1, SHARD, D), f32),
            dma((T,)), dma((T,)), dma((T, NY * NZ)), dma((T, NY * NZ)), dma((T,)), dma((T,)),
            dma((T, NX - 1)), dma((T, NX - 1)),
            dma((NZ,)), dma((NZ,)), dma((NZ, NY - 1)), dma((NZ, NY - 1)), dma((NZ,)), dma((NZ,)),
            dma((NZ,)), dma((NZ,)), dma((NZ, NY - 1)), dma((NZ, NY - 1)), dma((NZ,)), dma((NZ,)),
        ],
        compiler_params=pltpu.CompilerParams(
            collective_id=0, has_side_effects=True, vmem_limit_bytes=48 << 20
        ),
    )(
        pltpu.with_memory_space_constraint(patients, pltpu.HBM),
        pltpu.with_memory_space_constraint(centroids, pltpu.HBM),
    )
    return new, log.reshape(R)


def solution(mesh):
    return jax.shard_map(
        local,
        mesh=mesh,
        in_specs=(P("rows", None), P("cents", None)),
        out_specs=(P("cents", None), P("rows")),
        check_vma=False,
    )
```

```python
import functools
import math

import jax
import jax.numpy as jnp
from jax import lax
from jax.experimental import pallas as pl
from jax.experimental.pallas import tpu as pltpu
from jax.sharding import PartitionSpec as P

ITERS = 3
TAU = 0.05
LOG2E = math.log2(math.e)

NX, NY, NZ = 4, 4, 8
R = 2048
K = 2048
D = 256
HALF = K // 2
GROUP = HALF // NZ
SHARD = GROUP // NY
LANES = 128
CHUNKS = R // LANES
MESH = pl.DeviceIdType.MESH
Y_LAG = 7
G_LAG = 4
NT = (((1,), (1,)), ((), ()))


PEERS = [(dy, dz) for dz in (4, 3, 5, 2, 6, 1, 7, 0) for dy in (2, 1, 3, 0)][:-1]


def far_first(i):
    half = (i + 1) // 2
    return 4 + half * (1 - 2 * lax.rem(i, 2))


def kernel(
    ratio, p_hbm, c_hbm, new_ref, log_ref, p_ref, c_ref, t_even, t_odd, in_s,
    expo, col_b, row_b, acc, norm_b, peak8, factor,
    dense, pre, own, colbuf, total, rowpart, xbuf,
    low, numer, corebuf, ybuf, zsrc, zbuf,
    pre_s, pre_r, col_s, col_r, post_s, post_r, x_s, x_r,
    core_s, core_r, y_s, y_r, z_s, z_r, agz_s, agz_r, agy_s, agy_r, agc_s, agc_r,
):
    x = lax.axis_index("cents")
    rows = lax.axis_index("rows")
    core = lax.rem(rows, 2)
    z = lax.rem(rows // 2, NZ)
    y = rows // (2 * NZ)
    other = 1 - core

    def dev(dx=0, dy=0, dz=0, flip=False):
        yy = lax.rem(y + dy, NY)
        zz = lax.rem(z + dz, NZ)
        cc = other if flip else core
        return {"rows": (yy * NZ + zz) * 2 + cc, "cents": lax.rem(x + dx, NX)}

    def copy(src, dst, send, recv, to):
        return pltpu.make_async_remote_copy(
            src_ref=src, dst_ref=dst, send_sem=send, recv_sem=recv, device_id=to, device_id_type=MESH
        )

    fetch_c = pltpu.make_async_copy(c_hbm, c_ref, in_s.at[0])
    fetch_p = pltpu.make_async_copy(p_hbm, p_ref, in_s.at[1])
    fetch_c.start()
    fetch_p.start()

    barrier = pltpu.get_barrier_semaphore()

    for dy, dz in PEERS:
        pl.semaphore_signal(barrier, inc=1, device_id=dev(dy=dy, dz=dz), device_id_type=MESH)
    for dx in (2, 1, 3):
        pl.semaphore_signal(barrier, inc=1, device_id=dev(dx=dx), device_id_type=MESH)
    pl.semaphore_signal(barrier, inc=1, device_id=dev(flip=True), device_id_type=MESH)

    def norms(q, carry):
        at = pl.ds(pl.multiple_of(q * 256, 256), 256)
        cent = c_ref[at, :].astype(jnp.float32)
        norm_b[at, :] = jnp.broadcast_to(
            jnp.sum(cent * cent, axis=1, keepdims=True) * (LOG2E / TAU), (256, LANES)
        )
        return carry

    fetch_c.wait()
    lax.fori_loop(0, K // 256, norms, 0)
    fetch_p.wait()

    def block_lanes(b):
        return pl.ds(pl.multiple_of(b * 256, 256), 256)

    def score_part(q, b, buf):
        at = slice(q * 512, (q + 1) * 512)
        s = lax.dot_general(c_ref[at, :], p_ref[block_lanes(b), :], NT, preferred_element_type=jnp.float32)
        bias = norm_b[at, :]
        t = s * (2.0 * LOG2E / TAU) - jnp.concatenate([bias, bias], axis=1)
        buf[at, :] = t
        return jnp.max(t.reshape(64, 8, 256), axis=0)

    def exp_part(q, b, buf, top):
        at = slice(q * 512, (q + 1) * 512)
        expo[at, block_lanes(b)] = jnp.exp2(buf[at, :] - top)

    def set_peak(b, tops):
        top = jnp.max(jnp.maximum(jnp.maximum(tops[0], tops[1]), jnp.maximum(tops[2], tops[3])), axis=0, keepdims=True)
        peak8[:, block_lanes(b)] = jnp.broadcast_to(top, (8, 256))

    def step(b, buf, last):
        top = peak8[0:1, block_lanes(b - 1)]
        tops = []
        for q in range(4):
            tops.append(score_part(q, b, buf))
            exp_part(q, b - 1, last, top)
        set_peak(b, tops)

    set_peak(0, [score_part(q, 0, t_even) for q in range(4)])

    def pair(m, carry):
        step(2 * m + 1, t_odd, t_even)
        step(2 * m + 2, t_even, t_odd)
        return carry

    lax.fori_loop(0, R // 512 - 1, pair, 0)
    step(R // 256 - 1, t_odd, t_even)
    for q in range(4):
        exp_part(q, R // 256 - 1, t_odd, peak8[0:1, R - 256 :])

    def to_dense(src8, dst):
        for g in range(CHUNKS):
            dst[g : g + 1, :] = src8[0:1, g * LANES : (g + 1) * LANES]

    def to_lanes(value, dst8):
        for g in range(CHUNKS):
            dst8[:, g * LANES : (g + 1) * LANES] = jnp.broadcast_to(value[g : g + 1, :], (8, LANES))

    to_dense(peak8, rowpart.at[0])
    pl.semaphore_wait(barrier, NY * NZ - 1 + NX - 1 + 1)

    def x_exchange(t, meanwhile=lambda: None):
        xbuf[t, x] = rowpart[t]

        def one(dx):
            return copy(rowpart.at[t], xbuf.at[t, x], x_s.at[t, dx - 1], x_r.at[t, dx - 1], dev(dx=dx))

        for dx in (2, 1, 3):
            one(dx).start()
        meanwhile()
        for dx in (1, 3, 2):
            one(dx).wait_send()
        for dx in (1, 3, 2):
            one(dx).wait_recv()

    x_exchange(0)
    peak = jnp.maximum(jnp.maximum(xbuf[0, 0], xbuf[0, 1]), jnp.maximum(xbuf[0, 2], xbuf[0, 3]))
    factor[...] = jnp.exp2(rowpart[0] - peak)
    to_lanes(factor[...], row_b)

    ones = jnp.ones((8, LANES), jnp.float32)

    def lane_sums(h, t):
        for g in range(NZ):
            at = pl.ds(pl.multiple_of(h * HALF + g * LANES, LANES), LANES)
            s = lax.dot_general(
                ones, acc[at, :], NT, preferred_element_type=jnp.float32, precision=lax.Precision.HIGHEST
            )
            dense[t, h, g : g + 1, :] = s[0:1, :]

    def col_pass(h):
        r = [row_b[:, k * LANES : (k + 1) * LANES] for k in range(CHUNKS)]

        def body(q, carry):
            at = pl.ds(pl.multiple_of(h * HALF + q * 8, 8), 8)
            terms = [expo[at, k * LANES : (k + 1) * LANES] * r[k] for k in range(CHUNKS)]
            while len(terms) > 1:
                terms = [a + b for a, b in zip(terms[::2], terms[1::2])]
            acc[at, :] = terms[0]
            return carry

        lax.fori_loop(0, HALF // 8, body, 0, unroll=4)

    def row_pass(h, carry):
        def body(q, carry):
            at = pl.ds(pl.multiple_of(h * HALF + q * 8, 8), 8)
            c = col_b[at, :]
            return tuple(carry[k] + expo[at, k * LANES : (k + 1) * LANES] * c for k in range(CHUNKS))

        return lax.fori_loop(0, HALF // 8, body, carry, unroll=4)

    def pre_copy(t):
        return copy(dense.at[t, other], pre.at[t], pre_s.at[t], pre_r.at[t], dev(flip=True))

    def post_copy(t):
        return copy(total.at[t, core], total.at[t, core], post_s.at[t], post_r.at[t], dev(flip=True))

    def col_all(t):
        return copy(colbuf.at[t], colbuf.at[t], col_s.at[t], col_r.at[t], dev(dz=1))

    def col_send(t):
        pre_copy(t).wait_recv()
        own[t] = dense[t, core] + pre[t]
        for k, (dy, dz) in enumerate(PEERS):
            copy(own.at[t], colbuf.at[t, k], col_s.at[t], col_r.at[t], dev(dy=dy, dz=dz)).start()

    def col_finish(t):
        col_all(t).wait_recv()
        terms = [colbuf[t, k] for k in range(len(PEERS))] + [own[t]]
        while len(terms) > 1:
            terms = [a + b for a, b in zip(terms[::2], terms[1::2])]
        total[t, core] = terms[0]

    def col_drain(t):
        col_all(t).wait_send()
        pre_copy(t).wait_send()

    def scale_half(t, h):
        scale = ratio / jnp.maximum(total[t, h], 1.0)
        for g in range(NZ):
            at = pl.ds(pl.multiple_of(h * HALF + g * LANES, LANES), LANES)
            col_b[at, :] = jnp.broadcast_to(scale[g : g + 1, :], (LANES, LANES)).T

    def one_round(t, carry):
        col_pass(other)
        lane_sums(other, t)
        pre_copy(t).start()
        col_pass(core)
        lane_sums(core, t)
        col_send(t)
        col_finish(t)
        post_copy(t).start()
        scale_half(t, core)
        mass = row_pass(core, tuple(jnp.zeros((8, LANES), jnp.float32) for _ in range(CHUNKS)))
        post_copy(t).wait_recv()
        scale_half(t, other)
        mass = row_pass(other, mass)
        for g in range(CHUNKS):
            rowpart[t + 1, g : g + 1, :] = jnp.sum(mass[g], axis=0, keepdims=True)
        rowpart[t + 1] = rowpart[t + 1] * factor[...]

        def drain():
            col_drain(t)
            post_copy(t).wait_send()

        x_exchange(t + 1, drain)
        row_mass = (xbuf[t + 1, 0] + xbuf[t + 1, 1]) + (xbuf[t + 1, 2] + xbuf[t + 1, 3])
        log_ref[...] = -jnp.log(row_mass)
        to_lanes(factor[...] / row_mass, row_b)
        return carry

    lax.fori_loop(0, ITERS, one_round, 0)

    def core_copy(i):
        return copy(numer.at[i, 1], corebuf.at[i], core_s.at[i], core_r.at[i], dev(flip=True))

    def part_of(i, dy):
        return numer.at[i, 0, pl.ds(pl.multiple_of(lax.rem(y + dy, NY) * SHARD, SHARD), SHARD)]

    def y_copy(i, dy):
        return copy(part_of(i, dy), ybuf.at[i, dy - 1], y_s.at[i, dy - 1], y_r.at[i, dy - 1], dev(dy=dy))

    def z_copy(i):
        return copy(zsrc.at[i], zbuf.at[i], z_s.at[i], z_r.at[i], dev(dz=far_first(i)))

    def z_step(i):
        for dy in (1, 3, 2):
            y_copy(i, dy).wait_recv()
        zsrc[i] = (part_of(i, 0)[...] + ybuf[i, 0]) + (ybuf[i, 1] + ybuf[i, 2])

        @pl.when(i < NZ - 1)
        def _():
            z_copy(i).start()

    def group(i, carry):
        @pl.when(i < NZ)
        def _():
            to = lax.rem(z + far_first(i), NZ)
            for n, h in enumerate((core, other)):
                base = h * HALF + to * GROUP

                def body(q, carry):
                    at = pl.ds(pl.multiple_of(base + q * 16, 16), 16)
                    c = col_b[at, :]
                    terms = []
                    for k in range(CHUNKS):
                        lanes = slice(k * LANES, (k + 1) * LANES)
                        r = row_b[:, lanes]
                        w = expo[at, lanes] * jnp.concatenate([r, r], axis=0) * c
                        low[pl.ds(pl.multiple_of(n * GROUP + q * 16, 16), 16), lanes] = w.astype(jnp.bfloat16)
                        terms.append(w)
                    while len(terms) > 1:
                        terms = [a + b for a, b in zip(terms[::2], terms[1::2])]
                    acc[at, :] = terms[0]
                    return carry

                lax.fori_loop(0, GROUP // 16, body, 0, unroll=2)
            both = jnp.dot(low[...], p_ref[...], preferred_element_type=jnp.float32)
            numer[i, 0] = both[:GROUP]
            numer[i, 1] = both[GROUP:]
            core_copy(i).start()

        @pl.when(i >= 2)
        def _():
            j = i - 2
            core_copy(j).wait_recv()
            numer[j, 0] = numer[j, 0] + corebuf[j]
            for dy in (2, 1, 3):
                y_copy(j, dy).start()

        @pl.when(i >= Y_LAG)
        def _():
            z_step(i - Y_LAG)

        return carry

    lax.fori_loop(0, NZ + 2, group, 0)

    lane_sums(other, ITERS)
    pre_copy(ITERS).start()
    lane_sums(core, ITERS)
    z_step(NZ + 2 - Y_LAG)
    col_send(ITERS)

    def scatter(i, carry):
        z_step(i)
        return carry

    lax.fori_loop(NZ + 3 - Y_LAG, NZ, scatter, 0)

    col_finish(ITERS)
    weight = jnp.maximum(total[ITERS, core, pl.ds(z, 1), :], 1.0)
    norm_b[0:LANES, :] = jnp.broadcast_to(weight, (LANES, LANES)).T

    for i in range(NZ - 1):
        z_copy(i).wait_recv()
    numer_sum = zsrc[NZ - 1]
    for i in range(NZ - 1):
        numer_sum = numer_sum + zbuf[i]
    w = norm_b[pl.ds(pl.multiple_of(y * SHARD, SHARD), SHARD), :]

    def piece(zz, yy):
        return new_ref.at[pl.ds(pl.multiple_of(core * HALF + zz * GROUP + yy * SHARD, SHARD), SHARD)]

    mine = piece(z, y)
    mine[...] = numer_sum / jnp.concatenate([w, w], axis=1)

    def agz_copy(i):
        return copy(mine, mine, agz_s.at[i], agz_r.at[i], dev(dz=far_first(i)))

    def from_z(i):
        return lax.rem(z + NZ - far_first(i), NZ)

    def agy_copy(i, dy):
        part = piece(from_z(i), y)
        return copy(part, part, agy_s.at[i, dy - 1], agy_r.at[i, dy - 1], dev(dy=dy))

    def agc_copy(i):
        zz = from_z(i)
        part = new_ref.at[pl.ds(pl.multiple_of(core * HALF + zz * GROUP, GROUP), GROUP)]
        return copy(part, part, agc_s.at[0], agc_r.at[0], dev(flip=True))

    def gather_z(i, carry):
        agz_copy(i).start()
        return carry

    gather_z(0, 0)
    lax.fori_loop(0, NZ - 2, lambda n, carry: gather_z(NZ - 2 - n, carry), 0)

    def drain_scatter(i, carry):
        core_copy(i).wait_send()
        for dy in (1, 2, 3):
            y_copy(i, dy).wait_send()

        @pl.when(i < NZ - 1)
        def _():
            z_copy(i).wait_send()

        return carry

    def gather(n, carry):
        @pl.when(n < NZ)
        def _():
            i = NZ - 1 - n

            agz_copy(i).wait_recv()
            for dy in (2, 1, 3):
                agy_copy(i, dy).start()

        @pl.when(n >= G_LAG)
        def _():
            i = NZ - 1 - (n - G_LAG)
            for dy in (1, 3, 2):
                agy_copy(i, dy).wait_recv()
            agc_copy(i).start()

        return carry

    for dy in (2, 1, 3):
        agy_copy(NZ - 1, dy).start()
    col_drain(ITERS)
    lax.fori_loop(0, NZ, drain_scatter, 0)
    lax.fori_loop(1, NZ + G_LAG, gather, 0)

    def drain_gather(i, carry):
        for dy in (1, 2, 3):
            agy_copy(i, dy).wait_send()

        @pl.when(i < NZ - 1)
        def _():
            agz_copy(i).wait_send()

        return carry

    lax.fori_loop(0, NZ, drain_gather, 0)
    half = new_ref.at[pl.ds(pl.multiple_of(core * HALF, HALF), HALF)]
    whole = copy(half, half, agc_s.at[0], agc_r.at[0], dev(flip=True))
    whole.wait_send()
    whole.wait_recv()


def local(patients, centroids):
    ratio = float(R * NY * NZ * 2) / float(K * NX)
    f32 = jnp.float32
    T = ITERS + 1
    dma = pltpu.SemaphoreType.DMA
    vm = pltpu.VMEM
    new, log = pl.pallas_call(
        functools.partial(kernel, ratio),
        out_shape=(jax.ShapeDtypeStruct((K, D), f32), jax.ShapeDtypeStruct((CHUNKS, LANES), f32)),
        in_specs=[pl.BlockSpec(memory_space=pltpu.HBM)] * 2,
        out_specs=[pl.BlockSpec(memory_space=pltpu.VMEM)] * 2,
        scratch_shapes=[
            vm((R, D), jnp.bfloat16), vm((K, D), jnp.bfloat16), vm((K, 256), f32), vm((K, 256), f32), dma((2,)),
            vm((K, R), f32), vm((K, LANES), f32), vm((8, R), f32), vm((K, LANES), f32), vm((K, LANES), f32),
            vm((8, R), f32), vm((CHUNKS, LANES), f32),
            vm((T, 2, NZ, LANES), f32), vm((T, NZ, LANES), f32), vm((T, NZ, LANES), f32),
            vm((T, NY * NZ - 1, NZ, LANES), f32), vm((T, 2, NZ, LANES), f32),
            vm((T, CHUNKS, LANES), f32), vm((T, NX, CHUNKS, LANES), f32),
            vm((2 * GROUP, R), jnp.bfloat16), vm((NZ, 2, GROUP, D), f32), vm((NZ, GROUP, D), f32),
            vm((NZ, NY - 1, SHARD, D), f32), vm((NZ, SHARD, D), f32), vm((NZ - 1, SHARD, D), f32),
            dma((T,)), dma((T,)), dma((T,)), dma((T,)), dma((T,)), dma((T,)),
            dma((T, NX - 1)), dma((T, NX - 1)),
            dma((NZ,)), dma((NZ,)), dma((NZ, NY - 1)), dma((NZ, NY - 1)), dma((NZ,)), dma((NZ,)),
            dma((NZ,)), dma((NZ,)), dma((NZ, NY - 1)), dma((NZ, NY - 1)), dma((1,)), dma((1,)),
        ],
        compiler_params=pltpu.CompilerParams(
            collective_id=0, has_side_effects=True, vmem_limit_bytes=48 << 20
        ),
    )(
        pltpu.with_memory_space_constraint(patients, pltpu.HBM),
        pltpu.with_memory_space_constraint(centroids, pltpu.HBM),
    )
    return new, log.reshape(R)


def solution(mesh):
    return jax.shard_map(
        local,
        mesh=mesh,
        in_specs=(P("rows", None), P("cents", None)),
        out_specs=(P("cents", None), P("rows")),
        check_vma=False,
    )
```

```python
import functools
import math

import jax
import jax.numpy as jnp
from jax import lax
from jax.experimental import pallas as pl
from jax.experimental.pallas import tpu as pltpu
from jax.sharding import PartitionSpec as P

ITERS = 3
TAU = 0.05
LOG2E = math.log2(math.e)

NX, NY, NZ = 4, 4, 8
R = 2048
K = 2048
D = 256
HALF = K // 2
GROUP = HALF // NZ
SHARD = GROUP // NY
LANES = 128
CHUNKS = R // LANES
MESH = pl.DeviceIdType.MESH
Y_LAG = 7
G_LAG = 5
NT = (((1,), (1,)), ((), ()))


PEERS = [(dy, dz) for dz in (4, 3, 5, 2, 6, 1, 7, 0) for dy in (2, 1, 3, 0)][:-1]


def far_first(i):
    half = (i + 1) // 2
    return 4 + half * (1 - 2 * lax.rem(i, 2))


def kernel(
    ratio, p_hbm, c_hbm, new_ref, log_ref, p_ref, c_ref, t_even, t_odd, in_s,
    expo, col_b, row_b, acc, norm_b, peak8, factor,
    dense, pre, own, colbuf, total, rowpart, xbuf,
    low, numer, corebuf, ybuf, zsrc, zbuf,
    pre_s, pre_r, col_s, col_r, post_s, post_r, x_s, x_r,
    core_s, core_r, y_s, y_r, z_s, z_r, agz_s, agz_r, agy_s, agy_r, agc_s, agc_r,
):
    x = lax.axis_index("cents")
    rows = lax.axis_index("rows")
    core = lax.rem(rows, 2)
    z = lax.rem(rows // 2, NZ)
    y = rows // (2 * NZ)
    other = 1 - core

    def dev(dx=0, dy=0, dz=0, flip=False):
        yy = lax.rem(y + dy, NY)
        zz = lax.rem(z + dz, NZ)
        cc = other if flip else core
        return {"rows": (yy * NZ + zz) * 2 + cc, "cents": lax.rem(x + dx, NX)}

    def copy(src, dst, send, recv, to):
        return pltpu.make_async_remote_copy(
            src_ref=src, dst_ref=dst, send_sem=send, recv_sem=recv, device_id=to, device_id_type=MESH
        )

    fetch_c = pltpu.make_async_copy(c_hbm, c_ref, in_s.at[0])
    fetch_p = pltpu.make_async_copy(p_hbm, p_ref, in_s.at[1])
    fetch_c.start()
    fetch_p.start()

    barrier = pltpu.get_barrier_semaphore()

    for dy, dz in PEERS:
        pl.semaphore_signal(barrier, inc=1, device_id=dev(dy=dy, dz=dz), device_id_type=MESH)
    for dx in (2, 1, 3):
        pl.semaphore_signal(barrier, inc=1, device_id=dev(dx=dx), device_id_type=MESH)
    pl.semaphore_signal(barrier, inc=1, device_id=dev(flip=True), device_id_type=MESH)

    def norms(q, carry):
        at = pl.ds(pl.multiple_of(q * 256, 256), 256)
        cent = c_ref[at, :].astype(jnp.float32)
        norm_b[at, :] = jnp.broadcast_to(
            jnp.sum(cent * cent, axis=1, keepdims=True) * (LOG2E / TAU), (256, LANES)
        )
        return carry

    fetch_c.wait()
    lax.fori_loop(0, K // 256, norms, 0)
    fetch_p.wait()

    def block_lanes(b):
        return pl.ds(pl.multiple_of(b * 256, 256), 256)

    def score_part(q, b, buf):
        at = slice(q * 512, (q + 1) * 512)
        s = lax.dot_general(c_ref[at, :], p_ref[block_lanes(b), :], NT, preferred_element_type=jnp.float32)
        bias = norm_b[at, :]
        t = s * (2.0 * LOG2E / TAU) - jnp.concatenate([bias, bias], axis=1)
        buf[at, :] = t
        return jnp.max(t.reshape(64, 8, 256), axis=0)

    def exp_part(q, b, buf, top):
        at = slice(q * 512, (q + 1) * 512)
        expo[at, block_lanes(b)] = jnp.exp2(buf[at, :] - top)

    def set_peak(b, tops):
        top = jnp.max(jnp.maximum(jnp.maximum(tops[0], tops[1]), jnp.maximum(tops[2], tops[3])), axis=0, keepdims=True)
        peak8[:, block_lanes(b)] = jnp.broadcast_to(top, (8, 256))

    def step(b, buf, last):
        top = peak8[0:1, block_lanes(b - 1)]
        tops = []
        for q in range(4):
            tops.append(score_part(q, b, buf))
            exp_part(q, b - 1, last, top)
        set_peak(b, tops)

    set_peak(0, [score_part(q, 0, t_even) for q in range(4)])

    def pair(m, carry):
        step(2 * m + 1, t_odd, t_even)
        step(2 * m + 2, t_even, t_odd)
        return carry

    lax.fori_loop(0, R // 512 - 1, pair, 0)
    step(R // 256 - 1, t_odd, t_even)
    for q in range(4):
        exp_part(q, R // 256 - 1, t_odd, peak8[0:1, R - 256 :])

    def to_dense(src8, dst):
        for g in range(CHUNKS):
            dst[g : g + 1, :] = src8[0:1, g * LANES : (g + 1) * LANES]

    def to_lanes(value, dst8):
        for g in range(CHUNKS):
            dst8[:, g * LANES : (g + 1) * LANES] = jnp.broadcast_to(value[g : g + 1, :], (8, LANES))

    to_dense(peak8, rowpart.at[0])
    pl.semaphore_wait(barrier, NY * NZ - 1 + NX - 1 + 1)

    def x_exchange(t, meanwhile=lambda: None):
        xbuf[t, x] = rowpart[t]

        def one(dx):
            return copy(rowpart.at[t], xbuf.at[t, x], x_s.at[t, dx - 1], x_r.at[t, dx - 1], dev(dx=dx))

        for dx in (2, 1, 3):
            one(dx).start()
        meanwhile()
        for dx in (1, 3, 2):
            one(dx).wait_send()
        for dx in (1, 3, 2):
            one(dx).wait_recv()

    x_exchange(0)
    peak = jnp.maximum(jnp.maximum(xbuf[0, 0], xbuf[0, 1]), jnp.maximum(xbuf[0, 2], xbuf[0, 3]))
    factor[...] = jnp.exp2(rowpart[0] - peak)
    to_lanes(factor[...], row_b)

    def lane_sums(h, t):
        for g in range(NZ):
            at = pl.ds(pl.multiple_of(h * HALF + g * LANES, LANES), LANES)
            dense[t, h, g : g + 1, :] = jnp.sum(acc[at, :].T, axis=0, keepdims=True)

    def col_pass(h):
        r = [row_b[:, k * LANES : (k + 1) * LANES] for k in range(CHUNKS)]

        def body(q, carry):
            at = pl.ds(pl.multiple_of(h * HALF + q * 8, 8), 8)
            terms = [expo[at, k * LANES : (k + 1) * LANES] * r[k] for k in range(CHUNKS)]
            while len(terms) > 1:
                terms = [a + b for a, b in zip(terms[::2], terms[1::2])]
            acc[at, :] = terms[0]
            return carry

        lax.fori_loop(0, HALF // 8, body, 0, unroll=4)

    def row_pass(h, carry):
        def body(q, carry):
            at = pl.ds(pl.multiple_of(h * HALF + q * 8, 8), 8)
            c = col_b[at, :]
            return tuple(carry[k] + expo[at, k * LANES : (k + 1) * LANES] * c for k in range(CHUNKS))

        return lax.fori_loop(0, HALF // 8, body, carry, unroll=4)

    def pre_copy(t):
        return copy(dense.at[t, other], pre.at[t], pre_s.at[t], pre_r.at[t], dev(flip=True))

    def post_copy(t):
        return copy(total.at[t, core], total.at[t, core], post_s.at[t], post_r.at[t], dev(flip=True))

    def col_all(t):
        return copy(colbuf.at[t], colbuf.at[t], col_s.at[t], col_r.at[t], dev(dz=1))

    def col_send(t):
        pre_copy(t).wait_recv()
        own[t] = dense[t, core] + pre[t]
        for k, (dy, dz) in enumerate(PEERS):
            copy(own.at[t], colbuf.at[t, k], col_s.at[t], col_r.at[t], dev(dy=dy, dz=dz)).start()

    def col_finish(t):
        col_all(t).wait_recv()
        terms = [colbuf[t, k] for k in range(len(PEERS))] + [own[t]]
        while len(terms) > 1:
            terms = [a + b for a, b in zip(terms[::2], terms[1::2])]
        total[t, core] = terms[0]

    def col_drain(t):
        col_all(t).wait_send()
        pre_copy(t).wait_send()

    def scale_half(t, h):
        scale = ratio / jnp.maximum(total[t, h], 1.0)
        for g in range(NZ):
            at = pl.ds(pl.multiple_of(h * HALF + g * LANES, LANES), LANES)
            col_b[at, :] = jnp.broadcast_to(scale[g : g + 1, :], (LANES, LANES)).T

    def one_round(t, carry):
        col_pass(other)
        lane_sums(other, t)
        pre_copy(t).start()
        col_pass(core)
        lane_sums(core, t)
        col_send(t)
        col_finish(t)
        post_copy(t).start()
        scale_half(t, core)
        mass = row_pass(core, tuple(jnp.zeros((8, LANES), jnp.float32) for _ in range(CHUNKS)))
        post_copy(t).wait_recv()
        scale_half(t, other)
        mass = row_pass(other, mass)
        for g in range(CHUNKS):
            rowpart[t + 1, g : g + 1, :] = jnp.sum(mass[g], axis=0, keepdims=True)
        rowpart[t + 1] = rowpart[t + 1] * factor[...]

        def drain():
            col_drain(t)
            post_copy(t).wait_send()

        x_exchange(t + 1, drain)
        row_mass = (xbuf[t + 1, 0] + xbuf[t + 1, 1]) + (xbuf[t + 1, 2] + xbuf[t + 1, 3])
        log_ref[...] = -jnp.log(row_mass)
        to_lanes(factor[...] / row_mass, row_b)
        return carry

    lax.fori_loop(0, ITERS, one_round, 0)

    def core_copy(i):
        return copy(numer.at[i, 1], corebuf.at[i], core_s.at[i], core_r.at[i], dev(flip=True))

    def part_of(i, dy):
        return numer.at[i, 0, pl.ds(pl.multiple_of(lax.rem(y + dy, NY) * SHARD, SHARD), SHARD)]

    def y_copy(i, dy):
        return copy(part_of(i, dy), ybuf.at[i, dy - 1], y_s.at[i, dy - 1], y_r.at[i, dy - 1], dev(dy=dy))

    def z_copy(i):
        return copy(zsrc.at[i], zbuf.at[i], z_s.at[i], z_r.at[i], dev(dz=far_first(i)))

    def z_step(i):
        for dy in (1, 3, 2):
            y_copy(i, dy).wait_recv()
        zsrc[i] = (part_of(i, 0)[...] + ybuf[i, 0]) + (ybuf[i, 1] + ybuf[i, 2])

        @pl.when(i < NZ - 1)
        def _():
            z_copy(i).start()

    def group(i, carry):
        @pl.when(i < NZ)
        def _():
            to = lax.rem(z + far_first(i), NZ)
            for n, h in enumerate((core, other)):
                base = h * HALF + to * GROUP

                def body(q, carry):
                    at = pl.ds(pl.multiple_of(base + q * 16, 16), 16)
                    c = col_b[at, :]
                    terms = []
                    for k in range(CHUNKS):
                        lanes = slice(k * LANES, (k + 1) * LANES)
                        r = row_b[:, lanes]
                        w = expo[at, lanes] * jnp.concatenate([r, r], axis=0) * c
                        low[pl.ds(pl.multiple_of(n * GROUP + q * 16, 16), 16), lanes] = w.astype(jnp.bfloat16)
                        terms.append(w)
                    while len(terms) > 1:
                        terms = [a + b for a, b in zip(terms[::2], terms[1::2])]
                    acc[at, :] = terms[0]
                    return carry

                lax.fori_loop(0, GROUP // 16, body, 0, unroll=4)
            both = jnp.dot(low[...], p_ref[...], preferred_element_type=jnp.float32)
            numer[i, 0] = both[:GROUP]
            numer[i, 1] = both[GROUP:]
            core_copy(i).start()

        @pl.when(i >= 2)
        def _():
            j = i - 2
            core_copy(j).wait_recv()
            numer[j, 0] = numer[j, 0] + corebuf[j]
            for dy in (2, 1, 3):
                y_copy(j, dy).start()

        @pl.when(i >= Y_LAG)
        def _():
            z_step(i - Y_LAG)

        return carry

    lax.fori_loop(0, NZ + 2, group, 0)

    lane_sums(other, ITERS)
    pre_copy(ITERS).start()
    lane_sums(core, ITERS)
    z_step(NZ + 2 - Y_LAG)
    col_send(ITERS)

    def scatter(i, carry):
        z_step(i)
        return carry

    lax.fori_loop(NZ + 3 - Y_LAG, NZ, scatter, 0)

    col_finish(ITERS)
    weight = jnp.maximum(total[ITERS, core, pl.ds(z, 1), :], 1.0)
    norm_b[0:LANES, :] = jnp.broadcast_to(weight, (LANES, LANES)).T

    for i in range(NZ - 1):
        z_copy(i).wait_recv()
    numer_sum = zsrc[NZ - 1]
    for i in range(NZ - 1):
        numer_sum = numer_sum + zbuf[i]
    w = norm_b[pl.ds(pl.multiple_of(y * SHARD, SHARD), SHARD), :]

    def piece(zz, yy):
        return new_ref.at[pl.ds(pl.multiple_of(core * HALF + zz * GROUP + yy * SHARD, SHARD), SHARD)]

    mine = piece(z, y)
    mine[...] = numer_sum / jnp.concatenate([w, w], axis=1)

    def agz_copy(i):
        return copy(mine, mine, agz_s.at[i], agz_r.at[i], dev(dz=far_first(i)))

    def from_z(i):
        return lax.rem(z + NZ - far_first(i), NZ)

    def agy_copy(i, dy):
        part = piece(from_z(i), y)
        return copy(part, part, agy_s.at[i, dy - 1], agy_r.at[i, dy - 1], dev(dy=dy))

    def agc_copy(i):
        zz = from_z(i)
        part = new_ref.at[pl.ds(pl.multiple_of(core * HALF + zz * GROUP, GROUP), GROUP)]
        return copy(part, part, agc_s.at[0], agc_r.at[0], dev(flip=True))

    def gather_z(i, carry):
        agz_copy(i).start()
        return carry

    gather_z(0, 0)
    lax.fori_loop(0, NZ - 2, lambda n, carry: gather_z(NZ - 2 - n, carry), 0)

    def drain_scatter(i, carry):
        core_copy(i).wait_send()
        for dy in (1, 2, 3):
            y_copy(i, dy).wait_send()

        @pl.when(i < NZ - 1)
        def _():
            z_copy(i).wait_send()

        return carry

    def gather(n, carry):
        @pl.when(n < NZ)
        def _():
            i = NZ - 1 - n

            agz_copy(i).wait_recv()
            for dy in (2, 1, 3):
                agy_copy(i, dy).start()

        @pl.when(n >= G_LAG)
        def _():
            i = NZ - 1 - (n - G_LAG)
            for dy in (1, 3, 2):
                agy_copy(i, dy).wait_recv()
            agc_copy(i).start()

        return carry

    for dy in (2, 1, 3):
        agy_copy(NZ - 1, dy).start()
    col_drain(ITERS)
    lax.fori_loop(0, NZ, drain_scatter, 0)
    lax.fori_loop(1, NZ + G_LAG, gather, 0)

    def drain_gather(i, carry):
        for dy in (1, 2, 3):
            agy_copy(i, dy).wait_send()

        @pl.when(i < NZ - 1)
        def _():
            agz_copy(i).wait_send()

        return carry

    lax.fori_loop(0, NZ, drain_gather, 0)
    half = new_ref.at[pl.ds(pl.multiple_of(core * HALF, HALF), HALF)]
    whole = copy(half, half, agc_s.at[0], agc_r.at[0], dev(flip=True))
    whole.wait_send()
    whole.wait_recv()


def local(patients, centroids):
    ratio = float(R * NY * NZ * 2) / float(K * NX)
    f32 = jnp.float32
    T = ITERS + 1
    dma = pltpu.SemaphoreType.DMA
    vm = pltpu.VMEM
    new, log = pl.pallas_call(
        functools.partial(kernel, ratio),
        out_shape=(jax.ShapeDtypeStruct((K, D), f32), jax.ShapeDtypeStruct((CHUNKS, LANES), f32)),
        in_specs=[pl.BlockSpec(memory_space=pltpu.HBM)] * 2,
        out_specs=[pl.BlockSpec(memory_space=pltpu.VMEM)] * 2,
        scratch_shapes=[
            vm((R, D), jnp.bfloat16), vm((K, D), jnp.bfloat16), vm((K, 256), f32), vm((K, 256), f32), dma((2,)),
            vm((K, R), f32), vm((K, LANES), f32), vm((8, R), f32), vm((K, LANES), f32), vm((K, LANES), f32),
            vm((8, R), f32), vm((CHUNKS, LANES), f32),
            vm((T, 2, NZ, LANES), f32), vm((T, NZ, LANES), f32), vm((T, NZ, LANES), f32),
            vm((T, NY * NZ - 1, NZ, LANES), f32), vm((T, 2, NZ, LANES), f32),
            vm((T, CHUNKS, LANES), f32), vm((T, NX, CHUNKS, LANES), f32),
            vm((2 * GROUP, R), jnp.bfloat16), vm((NZ, 2, GROUP, D), f32), vm((NZ, GROUP, D), f32),
            vm((NZ, NY - 1, SHARD, D), f32), vm((NZ, SHARD, D), f32), vm((NZ - 1, SHARD, D), f32),
            dma((T,)), dma((T,)), dma((T,)), dma((T,)), dma((T,)), dma((T,)),
            dma((T, NX - 1)), dma((T, NX - 1)),
            dma((NZ,)), dma((NZ,)), dma((NZ, NY - 1)), dma((NZ, NY - 1)), dma((NZ,)), dma((NZ,)),
            dma((NZ,)), dma((NZ,)), dma((NZ, NY - 1)), dma((NZ, NY - 1)), dma((1,)), dma((1,)),
        ],
        compiler_params=pltpu.CompilerParams(
            collective_id=0, has_side_effects=True, vmem_limit_bytes=48 << 20
        ),
    )(
        pltpu.with_memory_space_constraint(patients, pltpu.HBM),
        pltpu.with_memory_space_constraint(centroids, pltpu.HBM),
    )
    return new, log.reshape(R)


def solution(mesh):
    return jax.shard_map(
        local,
        mesh=mesh,
        in_specs=(P("rows", None), P("cents", None)),
        out_specs=(P("cents", None), P("rows")),
        check_vma=False,
    )
```

```python
import functools
import math

import jax
import jax.numpy as jnp
from jax import lax
from jax.experimental import pallas as pl
from jax.experimental.pallas import tpu as pltpu
from jax.sharding import PartitionSpec as P

ITERS = 3
TAU = 0.05
LOG2E = math.log2(math.e)

NX, NY, NZ = 4, 4, 8
R = 2048
K = 2048
D = 256
HALF = K // 2
GROUP = HALF // NZ
SHARD = GROUP // NY
LANES = 128
CHUNKS = R // LANES
MESH = pl.DeviceIdType.MESH
Y_LAG = 7
G_LAG = 5
NT = (((1,), (1,)), ((), ()))


PEERS = [(dy, dz) for dz in (4, 3, 5, 2, 6, 1, 7, 0) for dy in (2, 1, 3, 0)][:-1]


def far_first(i):
    half = (i + 1) // 2
    return 4 + half * (1 - 2 * lax.rem(i, 2))


def kernel(
    ratio, p_hbm, c_hbm, new_ref, log_ref, p_ref, c_ref, t_even, t_odd, in_s,
    expo, col_b, row_b, acc, norm_b, peak8, factor,
    dense, pre, own, colbuf, total, rowpart, xbuf,
    low, numer, corebuf, ybuf, zsrc, zbuf, w_rows, w_buf,
    pre_s, pre_r, col_s, col_r, w_s, w_r, post_s, post_r, x_s, x_r,
    core_s, core_r, y_s, y_r, z_s, z_r, agz_s, agz_r, agy_s, agy_r, agc_s, agc_r,
):
    x = lax.axis_index("cents")
    rows = lax.axis_index("rows")
    core = lax.rem(rows, 2)
    z = lax.rem(rows // 2, NZ)
    y = rows // (2 * NZ)
    other = 1 - core

    def dev(dx=0, dy=0, dz=0, flip=False):
        yy = lax.rem(y + dy, NY)
        zz = lax.rem(z + dz, NZ)
        cc = other if flip else core
        return {"rows": (yy * NZ + zz) * 2 + cc, "cents": lax.rem(x + dx, NX)}

    def copy(src, dst, send, recv, to):
        return pltpu.make_async_remote_copy(
            src_ref=src, dst_ref=dst, send_sem=send, recv_sem=recv, device_id=to, device_id_type=MESH
        )

    fetch_c = pltpu.make_async_copy(c_hbm, c_ref, in_s.at[0])
    fetch_p = pltpu.make_async_copy(p_hbm, p_ref, in_s.at[1])
    fetch_c.start()
    fetch_p.start()

    barrier = pltpu.get_barrier_semaphore()

    for dy, dz in PEERS:
        pl.semaphore_signal(barrier, inc=1, device_id=dev(dy=dy, dz=dz), device_id_type=MESH)
    for dx in (2, 1, 3):
        pl.semaphore_signal(barrier, inc=1, device_id=dev(dx=dx), device_id_type=MESH)
    pl.semaphore_signal(barrier, inc=1, device_id=dev(flip=True), device_id_type=MESH)

    def norms(q, carry):
        at = pl.ds(pl.multiple_of(q * 256, 256), 256)
        cent = c_ref[at, :].astype(jnp.float32)
        norm_b[at, :] = jnp.broadcast_to(
            jnp.sum(cent * cent, axis=1, keepdims=True) * (LOG2E / TAU), (256, LANES)
        )
        return carry

    fetch_c.wait()
    lax.fori_loop(0, K // 256, norms, 0)
    fetch_p.wait()

    def block_lanes(b):
        return pl.ds(pl.multiple_of(b * 256, 256), 256)

    def score_part(q, b, buf):
        at = slice(q * 512, (q + 1) * 512)
        s = lax.dot_general(c_ref[at, :], p_ref[block_lanes(b), :], NT, preferred_element_type=jnp.float32)
        bias = norm_b[at, :]
        t = s * (2.0 * LOG2E / TAU) - jnp.concatenate([bias, bias], axis=1)
        buf[at, :] = t
        return jnp.max(t.reshape(64, 8, 256), axis=0)

    def exp_part(q, b, buf, top):
        at = slice(q * 512, (q + 1) * 512)
        expo[at, block_lanes(b)] = jnp.exp2(buf[at, :] - top)

    def set_peak(b, tops):
        top = jnp.max(jnp.maximum(jnp.maximum(tops[0], tops[1]), jnp.maximum(tops[2], tops[3])), axis=0, keepdims=True)
        peak8[:, block_lanes(b)] = jnp.broadcast_to(top, (8, 256))

    def step(b, buf, last):
        top = peak8[0:1, block_lanes(b - 1)]
        tops = []
        for q in range(4):
            tops.append(score_part(q, b, buf))
            exp_part(q, b - 1, last, top)
        set_peak(b, tops)

    set_peak(0, [score_part(q, 0, t_even) for q in range(4)])

    def pair(m, carry):
        step(2 * m + 1, t_odd, t_even)
        step(2 * m + 2, t_even, t_odd)
        return carry

    lax.fori_loop(0, R // 512 - 1, pair, 0)
    step(R // 256 - 1, t_odd, t_even)
    for q in range(4):
        exp_part(q, R // 256 - 1, t_odd, peak8[0:1, R - 256 :])

    def to_dense(src8, dst):
        for g in range(CHUNKS):
            dst[g : g + 1, :] = src8[0:1, g * LANES : (g + 1) * LANES]

    def to_lanes(value, dst8):
        for g in range(CHUNKS):
            dst8[:, g * LANES : (g + 1) * LANES] = jnp.broadcast_to(value[g : g + 1, :], (8, LANES))

    to_dense(peak8, rowpart.at[0])
    pl.semaphore_wait(barrier, NY * NZ - 1 + NX - 1 + 1)

    def x_exchange(t, meanwhile=lambda: None):
        xbuf[t, x] = rowpart[t]

        def one(dx):
            return copy(rowpart.at[t], xbuf.at[t, x], x_s.at[t, dx - 1], x_r.at[t, dx - 1], dev(dx=dx))

        for dx in (2, 1, 3):
            one(dx).start()
        meanwhile()
        for dx in (1, 3, 2):
            one(dx).wait_send()
        for dx in (1, 3, 2):
            one(dx).wait_recv()

    x_exchange(0)
    peak = jnp.maximum(jnp.maximum(xbuf[0, 0], xbuf[0, 1]), jnp.maximum(xbuf[0, 2], xbuf[0, 3]))
    factor[...] = jnp.exp2(rowpart[0] - peak)
    to_lanes(factor[...], row_b)

    def lane_sums(h, t):
        for g in range(NZ):
            at = pl.ds(pl.multiple_of(h * HALF + g * LANES, LANES), LANES)
            dense[t, h, g : g + 1, :] = jnp.sum(acc[at, :].T, axis=0, keepdims=True)

    def col_pass(h):
        r = [row_b[:, k * LANES : (k + 1) * LANES] for k in range(CHUNKS)]

        def body(q, carry):
            at = pl.ds(pl.multiple_of(h * HALF + q * 8, 8), 8)
            terms = [expo[at, k * LANES : (k + 1) * LANES] * r[k] for k in range(CHUNKS)]
            while len(terms) > 1:
                terms = [a + b for a, b in zip(terms[::2], terms[1::2])]
            acc[at, :] = terms[0]
            return carry

        lax.fori_loop(0, HALF // 8, body, 0, unroll=4)

    def row_pass(h, carry):
        def body(q, carry):
            at = pl.ds(pl.multiple_of(h * HALF + q * 8, 8), 8)
            c = col_b[at, :]
            return tuple(carry[k] + expo[at, k * LANES : (k + 1) * LANES] * c for k in range(CHUNKS))

        return lax.fori_loop(0, HALF // 8, body, carry, unroll=4)

    def pre_copy(t):
        return copy(dense.at[t, other], pre.at[t], pre_s.at[t], pre_r.at[t], dev(flip=True))

    def post_copy(t):
        return copy(total.at[t, core], total.at[t, core], post_s.at[t], post_r.at[t], dev(flip=True))

    def col_all(t):
        return copy(colbuf.at[t], colbuf.at[t], col_s.at[t], col_r.at[t], dev(dz=1))

    def col_send(t):
        pre_copy(t).wait_recv()
        own[t] = dense[t, core] + pre[t]
        for k, (dy, dz) in enumerate(PEERS):
            copy(own.at[t], colbuf.at[t, k], col_s.at[t], col_r.at[t], dev(dy=dy, dz=dz)).start()

    def col_finish(t):
        col_all(t).wait_recv()
        terms = [colbuf[t, k] for k in range(len(PEERS))] + [own[t]]
        while len(terms) > 1:
            terms = [a + b for a, b in zip(terms[::2], terms[1::2])]
        total[t, core] = terms[0]

    def col_drain(t):
        col_all(t).wait_send()
        pre_copy(t).wait_send()

    def scale_half(t, h):
        scale = ratio / jnp.maximum(total[t, h], 1.0)
        for g in range(NZ):
            at = pl.ds(pl.multiple_of(h * HALF + g * LANES, LANES), LANES)
            col_b[at, :] = jnp.broadcast_to(scale[g : g + 1, :], (LANES, LANES)).T

    def one_round(t, carry):
        col_pass(other)
        lane_sums(other, t)
        pre_copy(t).start()
        col_pass(core)
        lane_sums(core, t)
        col_send(t)
        col_finish(t)
        post_copy(t).start()
        scale_half(t, core)
        mass = row_pass(core, tuple(jnp.zeros((8, LANES), jnp.float32) for _ in range(CHUNKS)))
        post_copy(t).wait_recv()
        scale_half(t, other)
        mass = row_pass(other, mass)
        for g in range(CHUNKS):
            rowpart[t + 1, g : g + 1, :] = jnp.sum(mass[g], axis=0, keepdims=True)
        rowpart[t + 1] = rowpart[t + 1] * factor[...]

        def drain():
            col_drain(t)
            post_copy(t).wait_send()

        x_exchange(t + 1, drain)
        row_mass = (xbuf[t + 1, 0] + xbuf[t + 1, 1]) + (xbuf[t + 1, 2] + xbuf[t + 1, 3])
        log_ref[...] = -jnp.log(row_mass)
        to_lanes(factor[...] / row_mass, row_b)
        return carry

    lax.fori_loop(0, ITERS, one_round, 0)

    def core_copy(i):
        return copy(numer.at[i, 1], corebuf.at[i], core_s.at[i], core_r.at[i], dev(flip=True))

    def part_of(i, dy):
        return numer.at[i, 0, pl.ds(pl.multiple_of(lax.rem(y + dy, NY) * SHARD, SHARD), SHARD)]

    def y_copy(i, dy):
        return copy(part_of(i, dy), ybuf.at[i, dy - 1], y_s.at[i, dy - 1], y_r.at[i, dy - 1], dev(dy=dy))

    def z_copy(i):
        return copy(zsrc.at[i], zbuf.at[i], z_s.at[i], z_r.at[i], dev(dz=far_first(i)))

    def z_step(i):
        for dy in (1, 3, 2):
            y_copy(i, dy).wait_recv()
        zsrc[i] = (part_of(i, 0)[...] + ybuf[i, 0]) + (ybuf[i, 1] + ybuf[i, 2])

        @pl.when(i < NZ - 1)
        def _():
            z_copy(i).start()

    def group(i, carry):
        @pl.when(i < NZ)
        def _():
            to = lax.rem(z + far_first(i), NZ)
            for n, h in enumerate((core, other)):
                base = h * HALF + to * GROUP

                def body(q, carry):
                    at = pl.ds(pl.multiple_of(base + q * 16, 16), 16)
                    c = col_b[at, :]
                    terms = []
                    for k in range(CHUNKS):
                        lanes = slice(k * LANES, (k + 1) * LANES)
                        r = row_b[:, lanes]
                        w = expo[at, lanes] * jnp.concatenate([r, r], axis=0) * c
                        low[pl.ds(pl.multiple_of(n * GROUP + q * 16, 16), 16), lanes] = w.astype(jnp.bfloat16)
                        terms.append(w)
                    while len(terms) > 1:
                        terms = [a + b for a, b in zip(terms[::2], terms[1::2])]
                    acc[at, :] = terms[0]
                    return carry

                lax.fori_loop(0, GROUP // 16, body, 0, unroll=4)
            both = jnp.dot(low[...], p_ref[...], preferred_element_type=jnp.float32)
            numer[i, 0] = both[:GROUP]
            numer[i, 1] = both[GROUP:]
            core_copy(i).start()

        @pl.when(i >= 2)
        def _():
            j = i - 2
            core_copy(j).wait_recv()
            numer[j, 0] = numer[j, 0] + corebuf[j]
            for dy in (2, 1, 3):
                y_copy(j, dy).start()

        @pl.when(i >= Y_LAG)
        def _():
            z_step(i - Y_LAG)

        return carry

    lax.fori_loop(0, NZ + 2, group, 0)

    lane_sums(other, ITERS)
    pre_copy(ITERS).start()
    lane_sums(core, ITERS)
    for i in range(NZ + 2 - Y_LAG, NZ + 4 - Y_LAG):
        z_step(i)
    pre_copy(ITERS).wait_recv()
    weights = dense[ITERS, core] + pre[ITERS]
    for g in range(NZ):
        w_rows[g] = weights[g : g + 1, :]
    for k, (dy, dz) in enumerate(PEERS):
        copy(w_rows.at[lax.rem(z + dz, NZ)], w_buf.at[k], w_s, w_r, dev(dy=dy, dz=dz)).start()
    w_all = copy(w_buf, w_buf, w_s, w_r, dev(dz=1))

    def scatter(i, carry):
        z_step(i)
        return carry

    lax.fori_loop(NZ + 4 - Y_LAG, NZ, scatter, 0)

    w_all.wait_recv()
    weight = w_rows[z]
    for k in range(len(PEERS)):
        weight = weight + w_buf[k]
    weight = jnp.maximum(weight, 1.0)
    norm_b[0:LANES, :] = jnp.broadcast_to(weight, (LANES, LANES)).T

    for i in range(NZ - 1):
        z_copy(i).wait_recv()
    numer_sum = zsrc[NZ - 1]
    for i in range(NZ - 1):
        numer_sum = numer_sum + zbuf[i]
    w = norm_b[pl.ds(pl.multiple_of(y * SHARD, SHARD), SHARD), :]

    def piece(zz, yy):
        return new_ref.at[pl.ds(pl.multiple_of(core * HALF + zz * GROUP + yy * SHARD, SHARD), SHARD)]

    mine = piece(z, y)
    mine[...] = numer_sum / jnp.concatenate([w, w], axis=1)

    def agz_copy(i):
        return copy(mine, mine, agz_s.at[i], agz_r.at[i], dev(dz=far_first(i)))

    def from_z(i):
        return lax.rem(z + NZ - far_first(i), NZ)

    def agy_copy(i, dy):
        part = piece(from_z(i), y)
        return copy(part, part, agy_s.at[i, dy - 1], agy_r.at[i, dy - 1], dev(dy=dy))

    def agc_copy(i):
        zz = from_z(i)
        part = new_ref.at[pl.ds(pl.multiple_of(core * HALF + zz * GROUP, GROUP), GROUP)]
        return copy(part, part, agc_s.at[0], agc_r.at[0], dev(flip=True))

    def gather_z(i, carry):
        agz_copy(i).start()
        return carry

    gather_z(0, 0)
    lax.fori_loop(0, NZ - 2, lambda n, carry: gather_z(NZ - 2 - n, carry), 0)

    def drain_scatter(i, carry):
        core_copy(i).wait_send()
        for dy in (1, 2, 3):
            y_copy(i, dy).wait_send()

        @pl.when(i < NZ - 1)
        def _():
            z_copy(i).wait_send()

        return carry

    def gather(n, carry):
        @pl.when(n < NZ)
        def _():
            i = NZ - 1 - n

            agz_copy(i).wait_recv()
            for dy in (2, 1, 3):
                agy_copy(i, dy).start()

        @pl.when(n >= G_LAG)
        def _():
            i = NZ - 1 - (n - G_LAG)
            for dy in (1, 3, 2):
                agy_copy(i, dy).wait_recv()
            agc_copy(i).start()

        return carry

    for dy in (2, 1, 3):
        agy_copy(NZ - 1, dy).start()
    w_all.wait_send()
    pre_copy(ITERS).wait_send()
    lax.fori_loop(0, NZ, drain_scatter, 0)
    lax.fori_loop(1, NZ + G_LAG, gather, 0)

    def drain_gather(i, carry):
        for dy in (1, 2, 3):
            agy_copy(i, dy).wait_send()

        @pl.when(i < NZ - 1)
        def _():
            agz_copy(i).wait_send()

        return carry

    lax.fori_loop(0, NZ, drain_gather, 0)
    half = new_ref.at[pl.ds(pl.multiple_of(core * HALF, HALF), HALF)]
    whole = copy(half, half, agc_s.at[0], agc_r.at[0], dev(flip=True))
    whole.wait_send()
    whole.wait_recv()


def local(patients, centroids):
    ratio = float(R * NY * NZ * 2) / float(K * NX)
    f32 = jnp.float32
    T = ITERS + 1
    dma = pltpu.SemaphoreType.DMA
    vm = pltpu.VMEM
    new, log = pl.pallas_call(
        functools.partial(kernel, ratio),
        out_shape=(jax.ShapeDtypeStruct((K, D), f32), jax.ShapeDtypeStruct((CHUNKS, LANES), f32)),
        in_specs=[pl.BlockSpec(memory_space=pltpu.HBM)] * 2,
        out_specs=[pl.BlockSpec(memory_space=pltpu.VMEM)] * 2,
        scratch_shapes=[
            vm((R, D), jnp.bfloat16), vm((K, D), jnp.bfloat16), vm((K, 256), f32), vm((K, 256), f32), dma((2,)),
            vm((K, R), f32), vm((K, LANES), f32), vm((8, R), f32), vm((K, LANES), f32), vm((K, LANES), f32),
            vm((8, R), f32), vm((CHUNKS, LANES), f32),
            vm((T, 2, NZ, LANES), f32), vm((T, NZ, LANES), f32), vm((T, NZ, LANES), f32),
            vm((T, NY * NZ - 1, NZ, LANES), f32), vm((T, 2, NZ, LANES), f32),
            vm((T, CHUNKS, LANES), f32), vm((T, NX, CHUNKS, LANES), f32),
            vm((2 * GROUP, R), jnp.bfloat16), vm((NZ, 2, GROUP, D), f32), vm((NZ, GROUP, D), f32),
            vm((NZ, NY - 1, SHARD, D), f32), vm((NZ, SHARD, D), f32), vm((NZ - 1, SHARD, D), f32),
            vm((NZ, 1, LANES), f32), vm((NY * NZ - 1, 1, LANES), f32),
            dma((T,)), dma((T,)), dma((T,)), dma((T,)), dma, dma, dma((T,)), dma((T,)),
            dma((T, NX - 1)), dma((T, NX - 1)),
            dma((NZ,)), dma((NZ,)), dma((NZ, NY - 1)), dma((NZ, NY - 1)), dma((NZ,)), dma((NZ,)),
            dma((NZ,)), dma((NZ,)), dma((NZ, NY - 1)), dma((NZ, NY - 1)), dma((1,)), dma((1,)),
        ],
        compiler_params=pltpu.CompilerParams(
            collective_id=0, has_side_effects=True, vmem_limit_bytes=48 << 20
        ),
    )(
        pltpu.with_memory_space_constraint(patients, pltpu.HBM),
        pltpu.with_memory_space_constraint(centroids, pltpu.HBM),
    )
    return new, log.reshape(R)


def solution(mesh):
    return jax.shard_map(
        local,
        mesh=mesh,
        in_specs=(P("rows", None), P("cents", None)),
        out_specs=(P("cents", None), P("rows")),
        check_vma=False,
    )
```

```python
import functools
import math

import jax
import jax.numpy as jnp
from jax import lax
from jax.experimental import pallas as pl
from jax.experimental.pallas import tpu as pltpu
from jax.sharding import PartitionSpec as P

ITERS = 3
TAU = 0.05
LOG2E = math.log2(math.e)

NX, NY, NZ = 4, 4, 8
R = 2048
K = 2048
D = 256
HALF = K // 2
GROUP = HALF // NZ
SHARD = GROUP // NY
LANES = 128
CHUNKS = R // LANES
MESH = pl.DeviceIdType.MESH
Y_LAG = 7
G_LAG = 5
NT = (((1,), (1,)), ((), ()))


PEERS = [(dy, dz) for dz in (4, 3, 5, 2, 6, 1, 7, 0) for dy in (2, 1, 3, 0)][:-1]


def far_first(i):
    half = (i + 1) // 2
    return 4 + half * (1 - 2 * lax.rem(i, 2))


def kernel(
    ratio, p_hbm, c_hbm, new_ref, log_ref, p_ref, c_ref, t_even, t_odd, in_s,
    expo, col_b, row_b, acc, norm_b, peak8, factor,
    dense, pre, own, colbuf, total, rowpart, xbuf,
    low, numer, corebuf, ybuf, zsrc, zbuf, w_rows, w_buf,
    pre_s, pre_r, col_s, col_r, w_s, w_r, post_s, post_r, x_s, x_r,
    core_s, core_r, y_s, y_r, z_s, z_r, agz_s, agz_r, agy_s, agy_r, agc_s, agc_r,
):
    x = lax.axis_index("cents")
    rows = lax.axis_index("rows")
    core = lax.rem(rows, 2)
    z = lax.rem(rows // 2, NZ)
    y = rows // (2 * NZ)
    other = 1 - core

    def dev(dx=0, dy=0, dz=0, flip=False):
        yy = lax.rem(y + dy, NY)
        zz = lax.rem(z + dz, NZ)
        cc = other if flip else core
        return {"rows": (yy * NZ + zz) * 2 + cc, "cents": lax.rem(x + dx, NX)}

    def copy(src, dst, send, recv, to):
        return pltpu.make_async_remote_copy(
            src_ref=src, dst_ref=dst, send_sem=send, recv_sem=recv, device_id=to, device_id_type=MESH
        )

    fetch_c = pltpu.make_async_copy(c_hbm, c_ref, in_s.at[0])
    fetch_p = pltpu.make_async_copy(p_hbm, p_ref, in_s.at[1])
    fetch_c.start()
    fetch_p.start()

    barrier = pltpu.get_barrier_semaphore()

    for dy, dz in PEERS:
        pl.semaphore_signal(barrier, inc=1, device_id=dev(dy=dy, dz=dz), device_id_type=MESH)
    for dx in (2, 1, 3):
        pl.semaphore_signal(barrier, inc=1, device_id=dev(dx=dx), device_id_type=MESH)
    pl.semaphore_signal(barrier, inc=1, device_id=dev(flip=True), device_id_type=MESH)

    def norms(q, carry):
        at = pl.ds(pl.multiple_of(q * 256, 256), 256)
        cent = c_ref[at, :].astype(jnp.float32)
        norm_b[at, :] = jnp.broadcast_to(
            jnp.sum(cent * cent, axis=1, keepdims=True) * (LOG2E / TAU), (256, LANES)
        )
        return carry

    fetch_c.wait()
    lax.fori_loop(0, K // 256, norms, 0)
    fetch_p.wait()

    def block_lanes(b):
        return pl.ds(pl.multiple_of(b * 256, 256), 256)

    def score_part(q, b, buf):
        at = slice(q * 512, (q + 1) * 512)
        s = lax.dot_general(c_ref[at, :], p_ref[block_lanes(b), :], NT, preferred_element_type=jnp.float32)
        bias = norm_b[at, :]
        t = s * (2.0 * LOG2E / TAU) - jnp.concatenate([bias, bias], axis=1)
        buf[at, :] = t
        return jnp.max(t.reshape(64, 8, 256), axis=0)

    def exp_part(q, b, buf, top):
        at = slice(q * 512, (q + 1) * 512)
        expo[at, block_lanes(b)] = jnp.exp2(buf[at, :] - top)

    def set_peak(b, tops):
        top = jnp.max(jnp.maximum(jnp.maximum(tops[0], tops[1]), jnp.maximum(tops[2], tops[3])), axis=0, keepdims=True)
        peak8[:, block_lanes(b)] = jnp.broadcast_to(top, (8, 256))

    def step(b, buf, last):
        top = peak8[0:1, block_lanes(b - 1)]
        tops = []
        for q in range(4):
            tops.append(score_part(q, b, buf))
            exp_part(q, b - 1, last, top)
        set_peak(b, tops)

    set_peak(0, [score_part(q, 0, t_even) for q in range(4)])

    def pair(m, carry):
        step(2 * m + 1, t_odd, t_even)
        step(2 * m + 2, t_even, t_odd)
        return carry

    lax.fori_loop(0, R // 512 - 1, pair, 0)
    step(R // 256 - 1, t_odd, t_even)
    for q in range(4):
        exp_part(q, R // 256 - 1, t_odd, peak8[0:1, R - 256 :])

    def to_dense(src8, dst):
        for g in range(CHUNKS):
            dst[g : g + 1, :] = src8[0:1, g * LANES : (g + 1) * LANES]

    def to_lanes(value, dst8):
        for g in range(CHUNKS):
            dst8[:, g * LANES : (g + 1) * LANES] = jnp.broadcast_to(value[g : g + 1, :], (8, LANES))

    to_dense(peak8, rowpart.at[0])
    pl.semaphore_wait(barrier, NY * NZ - 1 + NX - 1 + 1)

    def x_exchange(t, meanwhile=lambda: None):
        xbuf[t, x] = rowpart[t]

        def one(dx):
            return copy(rowpart.at[t], xbuf.at[t, x], x_s.at[t, dx - 1], x_r.at[t, dx - 1], dev(dx=dx))

        for dx in (2, 1, 3):
            one(dx).start()
        meanwhile()
        for dx in (1, 3, 2):
            one(dx).wait_send()
        for dx in (1, 3, 2):
            one(dx).wait_recv()

    x_exchange(0)
    peak = jnp.maximum(jnp.maximum(xbuf[0, 0], xbuf[0, 1]), jnp.maximum(xbuf[0, 2], xbuf[0, 3]))
    factor[...] = jnp.exp2(rowpart[0] - peak)
    to_lanes(factor[...], row_b)

    def lane_sums(h, t):
        for g in range(NZ):
            at = pl.ds(pl.multiple_of(h * HALF + g * LANES, LANES), LANES)
            dense[t, h, g : g + 1, :] = jnp.sum(acc[at, :].T, axis=0, keepdims=True)

    def col_pass(h):
        r = [row_b[:, k * LANES : (k + 1) * LANES] for k in range(CHUNKS)]

        def body(q, carry):
            at = pl.ds(pl.multiple_of(h * HALF + q * 8, 8), 8)
            terms = [expo[at, k * LANES : (k + 1) * LANES] * r[k] for k in range(CHUNKS)]
            while len(terms) > 1:
                terms = [a + b for a, b in zip(terms[::2], terms[1::2])]
            acc[at, :] = terms[0]
            return carry

        lax.fori_loop(0, HALF // 8, body, 0, unroll=4)

    def row_pass(h, carry):
        def body(q, carry):
            at = pl.ds(pl.multiple_of(h * HALF + q * 8, 8), 8)
            c = col_b[at, :]
            return tuple(carry[k] + expo[at, k * LANES : (k + 1) * LANES] * c for k in range(CHUNKS))

        return lax.fori_loop(0, HALF // 8, body, carry, unroll=4)

    def pre_copy(t):
        return copy(dense.at[t, other], pre.at[t], pre_s.at[t], pre_r.at[t], dev(flip=True))

    def post_copy(t):
        return copy(total.at[t, core], total.at[t, core], post_s.at[t], post_r.at[t], dev(flip=True))

    def col_all(t):
        return copy(colbuf.at[t], colbuf.at[t], col_s.at[t], col_r.at[t], dev(dz=1))

    def col_send(t):
        pre_copy(t).wait_recv()
        own[t] = dense[t, core] + pre[t]
        for k, (dy, dz) in enumerate(PEERS):
            copy(own.at[t], colbuf.at[t, k], col_s.at[t], col_r.at[t], dev(dy=dy, dz=dz)).start()

    def col_finish(t):
        col_all(t).wait_recv()
        terms = [colbuf[t, k] for k in range(len(PEERS))] + [own[t]]
        while len(terms) > 1:
            terms = [a + b for a, b in zip(terms[::2], terms[1::2])]
        total[t, core] = terms[0]

    def col_drain(t):
        col_all(t).wait_send()
        pre_copy(t).wait_send()

    def scale_half(t, h):
        scale = ratio / jnp.maximum(total[t, h], 1.0)
        for g in range(NZ):
            at = pl.ds(pl.multiple_of(h * HALF + g * LANES, LANES), LANES)
            col_b[at, :] = jnp.broadcast_to(scale[g : g + 1, :], (LANES, LANES)).T

    def one_round(t, carry):
        col_pass(other)
        lane_sums(other, t)
        pre_copy(t).start()
        col_pass(core)
        lane_sums(core, t)
        col_send(t)
        col_finish(t)
        post_copy(t).start()
        scale_half(t, core)
        mass = row_pass(core, tuple(jnp.zeros((8, LANES), jnp.float32) for _ in range(CHUNKS)))
        post_copy(t).wait_recv()
        scale_half(t, other)
        mass = row_pass(other, mass)
        for g in range(CHUNKS):
            rowpart[t + 1, g : g + 1, :] = jnp.sum(mass[g], axis=0, keepdims=True)
        rowpart[t + 1] = rowpart[t + 1] * factor[...]

        def drain():
            col_drain(t)
            post_copy(t).wait_send()

        x_exchange(t + 1, drain)
        row_mass = (xbuf[t + 1, 0] + xbuf[t + 1, 1]) + (xbuf[t + 1, 2] + xbuf[t + 1, 3])
        log_ref[...] = row_mass
        to_lanes(factor[...] / row_mass, row_b)
        return carry

    lax.fori_loop(0, ITERS, one_round, 0)
    log_ref[...] = -jnp.log(log_ref[...])

    def core_copy(i):
        return copy(numer.at[i, 1], corebuf.at[i], core_s.at[i], core_r.at[i], dev(flip=True))

    def part_of(i, dy):
        return numer.at[i, 0, pl.ds(pl.multiple_of(lax.rem(y + dy, NY) * SHARD, SHARD), SHARD)]

    def y_copy(i, dy):
        return copy(part_of(i, dy), ybuf.at[i, dy - 1], y_s.at[i, dy - 1], y_r.at[i, dy - 1], dev(dy=dy))

    def z_copy(i):
        return copy(zsrc.at[i], zbuf.at[i], z_s.at[i], z_r.at[i], dev(dz=far_first(i)))

    def z_step(i):
        for dy in (1, 3, 2):
            y_copy(i, dy).wait_recv()
        zsrc[i] = (part_of(i, 0)[...] + ybuf[i, 0]) + (ybuf[i, 1] + ybuf[i, 2])

        @pl.when(i < NZ - 1)
        def _():
            z_copy(i).start()

    def group(i, carry):
        @pl.when(i < NZ)
        def _():
            to = lax.rem(z + far_first(i), NZ)
            for n, h in enumerate((core, other)):
                base = h * HALF + to * GROUP

                def body(q, carry):
                    at = pl.ds(pl.multiple_of(base + q * 16, 16), 16)
                    c = col_b[at, :]
                    terms = []
                    for k in range(CHUNKS):
                        lanes = slice(k * LANES, (k + 1) * LANES)
                        r = row_b[:, lanes]
                        w = expo[at, lanes] * jnp.concatenate([r, r], axis=0) * c
                        low[pl.ds(pl.multiple_of(n * GROUP + q * 16, 16), 16), lanes] = w.astype(jnp.bfloat16)
                        terms.append(w)
                    while len(terms) > 1:
                        terms = [a + b for a, b in zip(terms[::2], terms[1::2])]
                    acc[at, :] = terms[0]
                    return carry

                lax.fori_loop(0, GROUP // 16, body, 0, unroll=4)
            both = jnp.dot(low[...], p_ref[...], preferred_element_type=jnp.float32)
            numer[i, 0] = both[:GROUP]
            numer[i, 1] = both[GROUP:]
            core_copy(i).start()

        @pl.when(i >= 2)
        def _():
            j = i - 2
            core_copy(j).wait_recv()
            numer[j, 0] = numer[j, 0] + corebuf[j]
            for dy in (2, 1, 3):
                y_copy(j, dy).start()

        @pl.when(i >= Y_LAG)
        def _():
            z_step(i - Y_LAG)

        return carry

    lax.fori_loop(0, NZ + 2, group, 0)

    lane_sums(other, ITERS)
    pre_copy(ITERS).start()
    lane_sums(core, ITERS)
    for i in range(NZ + 2 - Y_LAG, NZ + 4 - Y_LAG):
        z_step(i)
    pre_copy(ITERS).wait_recv()
    weights = dense[ITERS, core] + pre[ITERS]
    for g in range(NZ):
        w_rows[g] = weights[g : g + 1, :]
    for k, (dy, dz) in enumerate(PEERS):
        copy(w_rows.at[lax.rem(z + dz, NZ)], w_buf.at[k], w_s, w_r, dev(dy=dy, dz=dz)).start()
    w_all = copy(w_buf, w_buf, w_s, w_r, dev(dz=1))

    def scatter(i, carry):
        z_step(i)
        return carry

    lax.fori_loop(NZ + 4 - Y_LAG, NZ, scatter, 0)

    w_all.wait_recv()
    weight = w_rows[z]
    for k in range(len(PEERS)):
        weight = weight + w_buf[k]
    weight = jnp.maximum(weight, 1.0)
    norm_b[0:LANES, :] = jnp.broadcast_to(weight, (LANES, LANES)).T

    for i in range(NZ - 1):
        z_copy(i).wait_recv()
    numer_sum = zsrc[NZ - 1]
    for i in range(NZ - 1):
        numer_sum = numer_sum + zbuf[i]
    w = norm_b[pl.ds(pl.multiple_of(y * SHARD, SHARD), SHARD), :]

    def piece(zz, yy):
        return new_ref.at[pl.ds(pl.multiple_of(core * HALF + zz * GROUP + yy * SHARD, SHARD), SHARD)]

    mine = piece(z, y)
    mine[...] = numer_sum / jnp.concatenate([w, w], axis=1)

    def agz_copy(i):
        return copy(mine, mine, agz_s.at[i], agz_r.at[i], dev(dz=far_first(i)))

    def from_z(i):
        return lax.rem(z + NZ - far_first(i), NZ)

    def agy_copy(i, dy):
        part = piece(from_z(i), y)
        return copy(part, part, agy_s.at[i, dy - 1], agy_r.at[i, dy - 1], dev(dy=dy))

    def agc_copy(i):
        zz = from_z(i)
        part = new_ref.at[pl.ds(pl.multiple_of(core * HALF + zz * GROUP, GROUP), GROUP)]
        return copy(part, part, agc_s.at[0], agc_r.at[0], dev(flip=True))

    def gather_z(i, carry):
        agz_copy(i).start()
        return carry

    gather_z(0, 0)
    lax.fori_loop(0, NZ - 2, lambda n, carry: gather_z(NZ - 2 - n, carry), 0)

    def drain_scatter(i, carry):
        core_copy(i).wait_send()
        for dy in (1, 2, 3):
            y_copy(i, dy).wait_send()

        @pl.when(i < NZ - 1)
        def _():
            z_copy(i).wait_send()

        return carry

    def gather(n, carry):
        @pl.when(n < NZ)
        def _():
            i = NZ - 1 - n

            agz_copy(i).wait_recv()
            for dy in (2, 1, 3):
                agy_copy(i, dy).start()

        @pl.when(n >= G_LAG)
        def _():
            i = NZ - 1 - (n - G_LAG)
            for dy in (1, 3, 2):
                agy_copy(i, dy).wait_recv()
            agc_copy(i).start()

        return carry

    for dy in (2, 1, 3):
        agy_copy(NZ - 1, dy).start()
    w_all.wait_send()
    pre_copy(ITERS).wait_send()
    lax.fori_loop(0, NZ, drain_scatter, 0)
    lax.fori_loop(1, NZ + G_LAG, gather, 0)

    def drain_gather(i, carry):
        for dy in (1, 2, 3):
            agy_copy(i, dy).wait_send()

        @pl.when(i < NZ - 1)
        def _():
            agz_copy(i).wait_send()

        return carry

    lax.fori_loop(0, NZ, drain_gather, 0)
    half = new_ref.at[pl.ds(pl.multiple_of(core * HALF, HALF), HALF)]
    whole = copy(half, half, agc_s.at[0], agc_r.at[0], dev(flip=True))
    whole.wait_send()
    whole.wait_recv()


def local(patients, centroids):
    ratio = float(R * NY * NZ * 2) / float(K * NX)
    f32 = jnp.float32
    T = ITERS + 1
    dma = pltpu.SemaphoreType.DMA
    vm = pltpu.VMEM
    new, log = pl.pallas_call(
        functools.partial(kernel, ratio),
        out_shape=(jax.ShapeDtypeStruct((K, D), f32), jax.ShapeDtypeStruct((CHUNKS, LANES), f32)),
        in_specs=[pl.BlockSpec(memory_space=pltpu.HBM)] * 2,
        out_specs=[pl.BlockSpec(memory_space=pltpu.VMEM)] * 2,
        scratch_shapes=[
            vm((R, D), jnp.bfloat16), vm((K, D), jnp.bfloat16), vm((K, 256), f32), vm((K, 256), f32), dma((2,)),
            vm((K, R), f32), vm((K, LANES), f32), vm((8, R), f32), vm((K, LANES), f32), vm((K, LANES), f32),
            vm((8, R), f32), vm((CHUNKS, LANES), f32),
            vm((T, 2, NZ, LANES), f32), vm((T, NZ, LANES), f32), vm((T, NZ, LANES), f32),
            vm((T, NY * NZ - 1, NZ, LANES), f32), vm((T, 2, NZ, LANES), f32),
            vm((T, CHUNKS, LANES), f32), vm((T, NX, CHUNKS, LANES), f32),
            vm((2 * GROUP, R), jnp.bfloat16), vm((NZ, 2, GROUP, D), f32), vm((NZ, GROUP, D), f32),
            vm((NZ, NY - 1, SHARD, D), f32), vm((NZ, SHARD, D), f32), vm((NZ - 1, SHARD, D), f32),
            vm((NZ, 1, LANES), f32), vm((NY * NZ - 1, 1, LANES), f32),
            dma((T,)), dma((T,)), dma((T,)), dma((T,)), dma, dma, dma((T,)), dma((T,)),
            dma((T, NX - 1)), dma((T, NX - 1)),
            dma((NZ,)), dma((NZ,)), dma((NZ, NY - 1)), dma((NZ, NY - 1)), dma((NZ,)), dma((NZ,)),
            dma((NZ,)), dma((NZ,)), dma((NZ, NY - 1)), dma((NZ, NY - 1)), dma((1,)), dma((1,)),
        ],
        compiler_params=pltpu.CompilerParams(
            collective_id=0, has_side_effects=True, vmem_limit_bytes=48 << 20
        ),
    )(
        pltpu.with_memory_space_constraint(patients, pltpu.HBM),
        pltpu.with_memory_space_constraint(centroids, pltpu.HBM),
    )
    return new, log.reshape(R)


def solution(mesh):
    return jax.shard_map(
        local,
        mesh=mesh,
        in_specs=(P("rows", None), P("cents", None)),
        out_specs=(P("cents", None), P("rows")),
        check_vma=False,
    )
```
